32 devices in a mesh: dp: 8 (over y, x, core), mp: 4 (over z).
Axes of the slice: x: 2, y: 2, z: 4, core: 2. Of those that a mesh axis runs over, the one named last changes fastest.
Arguments:
- tokens: bfloat16 [2048, 16, 512], P('mp', 'dp'), may hold values from -6 to 6
- lengths: int32 [16], P('dp'), may hold values from 256 to 2048, as said below
- gain_one: float32 [512], replicated, may hold values from 0.25 to 1.75
- shift_one: float32 [512], replicated, may hold values from -3 to 3
- w_query: bfloat16 [512, 512], P(None, 'mp'), may hold values from -0.375 to 0.375
- w_key: bfloat16 [512, 512], P(None, 'mp'), may hold values from -0.25 to 0.25
- w_value: bfloat16 [512, 512], P(None, 'mp'), may hold values from -0.25 to 0.25
- w_output: bfloat16 [512, 512], P('mp'), may hold values from -1 to 1
- gain_two: float32 [512], replicated, may hold values from 0.25 to 1.75
- shift_two: float32 [512], replicated, may hold values from -3 to 3
- w_up: bfloat16 [512, 2048], P(None, 'mp'), may hold values from -0.25 to 0.25
- w_down: bfloat16 [2048, 512], P('mp'), may hold values from -0.125 to 0.125
- cotangent: bfloat16 [2048, 16, 512], P('mp', 'dp'), may hold values from -6 to 6
Outputs:
- mixed: bfloat16 [2048, 16, 512], P('mp', 'dp')
- grad_tokens: float32 [2048, 16, 512], P('mp', 'dp')
- grad_query: float32 [512, 512], P(None, 'mp')
- grad_key: float32 [512, 512], P(None, 'mp')
- grad_value: float32 [512, 512], P(None, 'mp')
- grad_output: float32 [512, 512], P('mp')
- grad_up: float32 [512, 2048], P(None, 'mp')
- grad_down: float32 [2048, 512], P('mp')
- grad_gain_one: float32 [512], replicated
- grad_shift_one: float32 [512], replicated
- grad_gain_two: float32 [512], replicated
- grad_shift_two: float32 [512], replicated
The draws below stay inside these ranges and needn't reach their ends.
Inputs may be any that keep to these rules, and one draw needn't show every extreme that they name: `lengths`: in every group of 2 consecutive documents one has length 2048; the others vary from document to document.
All inputs are finite; a program needn't handle non-finite values.
Results may differ from the reference program's by a relative error of at most 0.018.
Values may be sent and summed in bfloat16 or wider, within the bound.
A program may use at most 256 MiB of HBM per device.

```python
import math
from functools import reduce
import jax
import jax.numpy as jnp
from jax import lax

D = 512
HEADS = 8
HEAD_DIM = 64
FF = 2048
BLOCK = 16
SEQ = 2048
DOCS_DEV = 2
DOCS = 16
N_MP = 4


def draw_lengths(key, part):
    key = jax.random.fold_in(key, 7)
    key_draw, key_pick = jax.random.split(key)
    lengths_drawn = jax.random.randint(key_draw, (DOCS,), SEQ // 8, SEQ + 1, dtype=jnp.int32)
    chosen = jax.random.randint(key_pick, (DOCS // DOCS_DEV,), 0, DOCS_DEV, dtype=jnp.int32)
    slot_idx = jnp.arange(DOCS, dtype=jnp.int32) % DOCS_DEV
    owner_idx = jnp.repeat(chosen, DOCS_DEV)
    return jnp.where(slot_idx == owner_idx, SEQ, lengths_drawn).astype(jnp.int32)


def block_scale(rng, shape, pieces, low, largest):
    def one(axis_at, shards_of):
        steps = jax.random.uniform(jax.random.fold_in(jax.random.fold_in(rng, 6), axis_at), (shards_of,), jnp.float32, low / len(pieces), largest / len(pieces))
        return jnp.repeat(jnp.exp(steps), shape[axis_at] // shards_of).reshape((-1,) + (1,) * (len(shape) - axis_at - 1))

    gain = one(*pieces[0])
    for cut in pieces[1:]:
        gain = gain * one(*cut)
    return gain


def noise(rng, extent, width, reach, shards=(), kind=jnp.bfloat16):
    factor_of = block_scale(rng, extent, shards, -0.22, 0.18) if shards else 1.0
    values = jax.random.normal(rng, extent, jnp.float32) * width * factor_of
    return jnp.minimum(jnp.maximum(values, -reach), reach).astype(kind)


def setup_inputs(seed: int = 0) -> dict:
    seeds = jax.random.split(jax.random.key(seed), 14)
    return {
        "tokens": noise(seeds[0], (SEQ, DOCS, D), 1.0, 6.0, ((0, 4), (1, 8))),
        "lengths": draw_lengths(jax.random.fold_in(seeds[13], 71), 0),
        "gain_one": jnp.clip(1.0 + 0.15 * jax.random.normal(seeds[2], (D,), jnp.float32), 0.25, 1.75),
        "shift_one": noise(seeds[3], (D,), 0.5, 3.0, (), jnp.float32),
        "w_query": noise(seeds[4], (D, D), (D // 2) ** -0.5, 0.375, ((1, 4),)),
        "w_key": noise(seeds[5], (D, D), D ** -0.5, 0.25, ((1, 4),)),
        "w_value": noise(seeds[6], (D, D), D ** -0.5, 0.25, ((1, 4),)),
        "w_output": noise(seeds[7], (D, D), (D // 16) ** -0.5, 1.0, ((0, 4),)),
        "gain_two": jnp.clip(1.0 + 0.15 * jax.random.normal(seeds[8], (D,), jnp.float32), 0.25, 1.75),
        "shift_two": noise(seeds[9], (D,), 0.5, 3.0, (), jnp.float32),
        "w_up": noise(seeds[10], (D, FF), D ** -0.5, 0.25, ((1, 4),)),
        "w_down": noise(seeds[11], (FF, D), FF ** -0.5, 0.125, ((0, 4),)),
        "cotangent": noise(seeds[12], (SEQ, DOCS, D), 1.0, 6.0, ((0, 4), (1, 8))),
    }


@jax.custom_vjp
def low(v):
    return lax.optimization_barrier(v.astype(jnp.bfloat16)).astype(jnp.float32)

@jax.custom_vjp
def low_back(v):
    return v

def low_keep(v):
    return (low(v), None)

def low_pass(kept, grad):
    return (grad,)

def back_keep(v):
    return (v, None)

def back_low(kept, grad):
    return (low(grad),)
low.defvjp(low_keep, low_pass)
low_back.defvjp(back_keep, back_low)

def layer_norm(values, gain_vec, shift_vec):
    row_mean = lax.optimization_barrier(jnp.mean(values, axis=-1, keepdims=True))
    centered = values - row_mean
    variance = lax.optimization_barrier(jnp.mean(centered * centered, axis=-1, keepdims=True))
    return centered * lax.rsqrt(variance + 1e-05) * gain_vec + shift_vec

def sibling(array):
    shaped = array.reshape((array.shape[0] // 2, 2) + array.shape[1:])
    return jnp.flip(shaped, axis=1).reshape(array.shape)

def upsample(array, stride):
    wide = jnp.broadcast_to(array[:, None], (array.shape[0], stride) + array.shape[1:])
    return wide.reshape((array.shape[0] * stride,) + array.shape[1:])

def hier_attend(queries, key_rows, value_rows, live_mask, span):
    length, head_count, head_size = queries.shape
    levels = (length // span).bit_length() - 1
    scaling = head_size ** (-0.5)
    row_tops, row_sums, row_nums = ([], [], [])
    for level_idx in range(levels):
        stride = 2 ** level_idx
        coarse = length // stride
        blocks = coarse // span
        counts = lax.optimization_barrier(jnp.sum(live_mask.reshape(coarse, stride), axis=1))
        safe_count = jnp.maximum(counts, 1.0)
        query_mean = lax.optimization_barrier(jnp.mean(queries.reshape(coarse, stride, head_count, head_size), axis=1))
        key_mean = lax.optimization_barrier(jnp.sum((key_rows * live_mask[:, None, None]).reshape(coarse, stride, head_count, head_size), axis=1)) / safe_count[:, None, None]
        value_mean = lax.optimization_barrier(jnp.sum((value_rows * live_mask[:, None, None]).reshape(coarse, stride, head_count, head_size), axis=1)) / safe_count[:, None, None]
        query_blocks = query_mean.reshape(blocks, span, head_count, head_size)
        key_blocks = key_mean.reshape(blocks, span, head_count, head_size)
        value_blocks = value_mean.reshape(blocks, span, head_count, head_size)
        count_blocks = counts.reshape(blocks, span)
        if level_idx == 0:
            key_set = jnp.concatenate([key_blocks, sibling(key_blocks)], axis=1)
            value_set = jnp.concatenate([value_blocks, sibling(value_blocks)], axis=1)
            count_set = jnp.concatenate([count_blocks, sibling(count_blocks)], axis=1)
        else:
            key_set = sibling(key_blocks)
            value_set = sibling(value_blocks)
            count_set = sibling(count_blocks)
        score = jnp.einsum('bqhe,bkhe->bhqk', query_blocks, key_set, precision=lax.Precision.HIGHEST) * scaling
        present = (count_set > 0.0)[:, None, None, :]
        score = jnp.where(present, score, -1e+30)
        row_top = lax.optimization_barrier(jnp.max(score, axis=-1))
        weight = count_set[:, None, None, :] * jnp.exp(score - row_top[..., None])
        row_sum = lax.optimization_barrier(jnp.sum(weight, axis=-1))
        row_num = jnp.einsum('bhqk,bkhe->bqhe', weight, value_set, precision=lax.Precision.HIGHEST)
        row_top = jnp.transpose(row_top, (0, 2, 1)).reshape(coarse, head_count)
        row_sum = jnp.transpose(row_sum, (0, 2, 1)).reshape(coarse, head_count)
        row_num = row_num.reshape(coarse, head_count, head_size)
        row_tops.append(upsample(row_top, stride))
        row_sums.append(upsample(row_sum, stride))
        row_nums.append(upsample(row_num, stride))
    overall = reduce(jnp.maximum, row_tops)
    total_sum = jnp.zeros_like(overall)
    total_num = jnp.zeros_like(queries)
    for level_idx in range(levels):
        factor = jnp.exp(row_tops[level_idx] - overall)
        total_sum = total_sum + row_sums[level_idx] * factor
        total_num = total_num + row_nums[level_idx] * factor[..., None]
    return total_num / total_sum[..., None]

def attend_one(queries, key_rows, value_rows, live_mask):
    return hier_attend(queries, key_rows, value_rows, live_mask, BLOCK)

def forward(params, block_in, live_mask):
    gain_one, shift_one, w_query, w_key, w_value, w_output, gain_two, shift_two, w_up, w_down = params
    length, doc_count, width_all = block_in.shape
    head_width = HEADS // N_MP * HEAD_DIM
    inner_width = FF // N_MP
    upper_level = lax.Precision.HIGHEST
    normed_one = low(layer_norm(block_in, gain_one, shift_one))
    attn_sum = jnp.zeros_like(block_in)
    for part_idx in range(N_MP):
        column_total = slice(part_idx * head_width, (part_idx + 1) * head_width)
        incoming_rows = low_back(normed_one)

        def project(complete_weight):
            built_result = jnp.einsum('gix,xh->gih', incoming_rows, complete_weight[:, column_total], precision=upper_level)
            return low(low_back(built_result)).reshape(length, doc_count, HEADS // N_MP, HEAD_DIM)
        context = jax.vmap(attend_one, in_axes=(1, 1, 1, 1), out_axes=1)(project(w_query), project(w_key), project(w_value), live_mask)
        context = low(context.reshape(length, doc_count, head_width))
        attn_sum = attn_sum + low(jnp.einsum('snw,wd->snd', context, w_output[column_total, :], precision=upper_level))
    middle = block_in + low_back(attn_sum)
    normed_two = low(layer_norm(middle, gain_two, shift_two))
    ffn_sum = jnp.zeros_like(block_in)
    for part_idx in range(N_MP):
        ff_columns = slice(part_idx * inner_width, (part_idx + 1) * inner_width)
        incoming_rows = low_back(normed_two)
        pre_act = low_back(jnp.einsum('snd,df->snf', incoming_rows, w_up[:, ff_columns], precision=upper_level))
        active = low(jax.nn.gelu(pre_act, approximate=False))
        ffn_sum = ffn_sum + low(jnp.einsum('snf,fd->snd', active, w_down[ff_columns, :], precision=upper_level))
    return middle + low_back(ffn_sum)

def reference(tokens, lengths, gain_one, shift_one, w_query, w_key, w_value, w_output, gain_two, shift_two, w_up, w_down, cotangent):
    params = tuple((item.astype(jnp.float32) for item in (gain_one, shift_one, w_query, w_key, w_value, w_output, gain_two, shift_two, w_up, w_down)))
    per_round = math.gcd(DOCS, max(1, 4096 // SEQ))
    rounds = DOCS // per_round

    def to_rounds(array):
        return jnp.moveaxis(array.astype(jnp.float32).reshape(SEQ, rounds, per_round, D), 1, 0)
    lens_all = lengths.reshape(rounds, per_round)

    def one_round(totals, inputs):
        block_in, grad_in, lens_now = inputs
        live_mask = (jnp.arange(SEQ, dtype=jnp.int32)[:, None] < lens_now[None, :]).astype(jnp.float32)

        def wrapped(prm, blk):
            return forward(prm, blk, live_mask)
        result, pullback = jax.vjp(wrapped, params, block_in)
        grads, grad_block = pullback(grad_in)
        totals = jax.tree.map(jnp.add, totals, grads)
        return (totals, (result.astype(jnp.bfloat16), grad_block))
    initial = jax.tree.map(jnp.zeros_like, params)
    summed, (results, grads_in) = lax.scan(one_round, initial, (to_rounds(tokens), to_rounds(cotangent), lens_all))
    mixed = jnp.moveaxis(results, 0, 1).reshape(SEQ, DOCS, D)
    grad_tokens = jnp.moveaxis(grads_in, 0, 1).reshape(SEQ, DOCS, D)
    return (mixed, grad_tokens, summed[2], summed[3], summed[4], summed[5], summed[8], summed[9], summed[0], summed[1], summed[6], summed[7])
```

```python
import types

import jax
import jax.numpy as jnp
from jax import lax
from jax.experimental import pallas as pl
from jax.experimental.pallas import tpu as pltpu
from jax.sharding import PartitionSpec as P

HD = 64
BLK = 16
NEG = -1e30
FLOOR = -1e29
EPS = 1e-05
LOC = 512
ND = 2
D = 512
FF = 2048
NMP = 4
T = ND * LOC
HEADS = D // HD
LEVELS = 7
LOCAL_LEVELS = 5
EXT = 1024
RT = 256
G = [LOC >> lev for lev in range(LEVELS)]
OFF = [sum(G[:lev]) for lev in range(LEVELS)]
bf16 = jnp.bfloat16
f32 = jnp.float32
i32 = jnp.int32


def dot(a, b, ca=1, cb=0):
    return lax.dot_general(a, b, (((ca,), (cb,)), ((), ())), preferred_element_type=f32)


def iota(shape, axis):
    return lax.broadcasted_iota(i32, shape, axis)


def loop(n, body):
    lax.fori_loop(0, n, lambda i, c: (body(i), c)[1], 0)


def rows_at(i, size):
    return pl.ds(pl.multiple_of(i * size, size), size)


def own_groups(e):
    size = jnp.zeros_like(e)
    start = jnp.zeros_like(e)
    for lev in range(LEVELS):
        here = (e >= OFF[lev]) & (e < OFF[lev] + G[lev])
        size = jnp.where(here, 1 << lev, size)
        start = jnp.where(here, (e - OFF[lev]) << lev, start)
    return size, start


def key_groups(e, z):
    size, start = own_groups(e)
    start = start + z * LOC
    near = z + 1 - 2 * lax.rem(z, 2)
    far = 1 - z // 2
    size = jnp.where(e >= OFF[5], 32, size)
    start = jnp.where(e >= OFF[5], near * LOC + (e - OFF[5]) * 32, start)
    size = jnp.where(e >= OFF[6], 64, size)
    start = jnp.where(e >= OFF[6], far * 2 * LOC + (e - OFF[6]) * 64, start)
    return size, start


def count_live(size, start, length):
    return jnp.clip(length - start, 0, size).astype(f32)


def build_tables(r, z):
    for d in range(ND):
        length = r.lens[d]

        def chunk(c, d=d, length=length):
            at = pl.ds(pl.multiple_of(d * EXT + c * 128, 128), 128)
            e_col = iota((128, 128), 0) + c * 128
            size, start = key_groups(e_col, z)
            r.cc[at, :] = count_live(size, start, length).astype(bf16)
            e_row = iota((1, 128), 1) + c * 128
            size, start = key_groups(e_row, z)
            dead = count_live(size, start, length)
            q_blk, k_blk = e_col // BLK, jnp.broadcast_to(e_row // BLK, (128, 128))
            span = jnp.where(q_blk // 2 == k_blk // 2, 0.0, NEG)
            same = jnp.where(q_blk == k_blk, 0.0, NEG)
            cross = jnp.where(q_blk == k_blk, NEG, span)
            bias = jnp.where(e_col < LOC, span, jnp.where(e_col < OFF[5], cross, same))
            r.bias[at, :] = jnp.where(jnp.broadcast_to(dead, (128, 128)) > 0.0, bias, NEG)

        loop(EXT // 128, chunk)


def build_maps(r):
    def tile(c):
        rows = rows_at(c, 128)
        size, start = own_groups(iota((128, LOC), 0) + c * 128 + LOC)
        pos = iota((128, LOC), 1)
        r.pool[rows, :] = ((pos >= start) & (pos < start + size)).astype(f32).astype(bf16)
        size, start = own_groups(iota((128, EXT - LOC), 1) + LOC)
        pos = iota((128, EXT - LOC), 0) + c * 128
        r.unpool[rows, :] = ((pos >= start) & (pos < start + size)).astype(f32).astype(bf16)

    loop((EXT - LOC) // 128, tile)


def inv_counts(r, z, d):
    e = iota((EXT - LOC, 128), 0) + LOC
    size, start = own_groups(e)
    cnt = count_live(size, start + z * LOC, r.lens[d])
    return 1.0 / jnp.maximum(cnt, 1.0), 1.0 / jnp.maximum(size, 1).astype(f32)


def wide(col):
    return jnp.concatenate([col] * (D // 128), axis=1)


def live_rows(r, z, d, first, count):
    pos = iota((count, D), 0) + first + z * LOC
    return pos < r.lens[d]


def stats(v):
    mean = jnp.mean(v, axis=-1, keepdims=True)
    cen = v - mean
    var = jnp.mean(cen * cen, axis=-1, keepdims=True)
    return cen, lax.rsqrt(var + EPS)


def norm_one(r):
    def tile(t):
        rows = rows_at(t, RT)
        cen, rstd = stats(r.x[rows, :].astype(f32))
        r.h1[rows, :] = (cen * rstd * r.g1[...] + r.b1[...]).astype(bf16)

    loop(T // RT, tile)


def ext_rows(d, off, count):
    return pl.ds(d * EXT + off, count)


def project(r, z):
    per = LOC // RT
    for d in range(ND):

        def tile(t, d=d):
            rows = pl.ds(pl.multiple_of(d * LOC + t * RT, RT), RT)
            at = pl.ds(pl.multiple_of(d * EXT + t * RT, RT), RT)
            h = r.h1[rows, :]
            live = live_rows(r, z, d, t * RT, RT)
            q = dot(h, r.wqkv[:, 0:D]).astype(bf16).astype(f32)
            r.qe[at, :] = (q * (HD**-0.5)).astype(bf16)
            k = dot(h, r.wqkv[:, D : 2 * D])
            r.ke[at, :] = jnp.where(live, k, 0.0).astype(bf16)
            v = dot(h, r.wqkv[:, 2 * D : 3 * D])
            r.ve[at, :] = jnp.where(live, v, 0.0).astype(bf16)

        loop(per, tile)


def pool_levels(r, z):
    keep = OFF[5] - LOC
    for d in range(ND):
        inv, inv_size = inv_counts(r, z, d)
        fine = ext_rows(d, 0, LOC)
        coarse = ext_rows(d, LOC, LOC)
        r.qe[coarse, :] = (dot(r.pool[...], r.qe[fine, :]) * wide(inv_size)).astype(bf16)
        k = dot(r.pool[...], r.ke[fine, :]) * wide(inv)
        v = dot(r.pool[...], r.ve[fine, :])
        r.ke[ext_rows(d, LOC, keep), :] = k[:keep].astype(bf16)
        r.ve[ext_rows(d, LOC, keep), :] = v[:keep].astype(bf16)
        r.sums[pl.ds(d * 48, 24), :] = k[keep : keep + 24]
        r.sums[pl.ds(d * 48 + 24, 24), :] = v[keep : keep + 24]


def place_remote(r):
    for d in range(ND):
        r.ke[ext_rows(d, OFF[5], 32), :] = r.rem[pl.ds(d * 64, 32), :].astype(bf16)
        r.ve[ext_rows(d, OFF[5], 32), :] = r.rem[pl.ds(d * 64 + 32, 32), :].astype(bf16)


def split_heads(pair):
    first = iota(pair.shape, 1) < HD
    zero = jnp.zeros_like(pair)
    return jnp.concatenate([jnp.where(first, pair, zero), jnp.where(first, zero, pair)], axis=0)


def count_lanes(cc, d, p):
    lane = iota(cc.shape, 1)
    zero = jnp.zeros_like(cc)
    a = jnp.where(lane == d * HEADS + 2 * p, cc, zero)
    b = jnp.where(lane == d * HEADS + 2 * p + 1, cc, zero)
    return jnp.concatenate([a, b], axis=0)


def attend_chunk(r, c):
    lane = iota((128, 128), 1)
    tops = jnp.zeros((128, 128), f32)
    sums = jnp.zeros((128, 128), f32)
    for d in range(ND):
        at = pl.ds(pl.multiple_of(d * EXT + c * 128, 128), 128)
        bias = r.bias[at, :]
        cc = r.cc[at, :]
        for p in range(HEADS // 2):
            lanes = pl.ds(p * 128, 128)
            s = dot(r.qe[at, lanes], split_heads(r.ke[at, lanes]), 1, 1)
            parts = []
            for j in range(2):
                sj = s[:, j * 128 : (j + 1) * 128] + bias
                top = jnp.maximum(jnp.max(sj, axis=1, keepdims=True), FLOOR)
                parts.append(jnp.exp(sj - top))
                tops = jnp.where(lane == d * HEADS + 2 * p + j, top, tops)
            e = jnp.concatenate(parts, axis=1).astype(bf16)
            slot = pl.ds(pl.multiple_of(((c * ND + d) * 4 + p) * 128, 128), 128)
            r.wts[slot, :] = e
            vo = jnp.concatenate([split_heads(r.ve[at, lanes]), count_lanes(cc, d, p)], axis=1)
            o = dot(e, vo)
            r.num[at, lanes] = o[:, :128]
            sums = sums + o[:, 128:]
    here = rows_at(c, 128)
    r.tops[here, :] = tops
    r.sumz[here, :] = sums


def combine_sums(r):
    last = pl.ds(OFF[6], G[6])
    top = r.tops[last, :]
    tot = r.sumz[last, :]
    for lev in range(LEVELS - 2, -1, -1):
        n = G[lev]
        for half in range(2):
            r.up[pl.ds(half, n // 2, stride=2), :] = top
            r.up2[pl.ds(half, n // 2, stride=2), :] = tot
        at = pl.ds(OFF[lev], n)
        up_top = r.up[pl.ds(0, n), :]
        own = r.tops[at, :]
        top = jnp.maximum(own, up_top)
        a = jnp.exp(own - top)
        b = jnp.exp(up_top - top)
        tot = a * r.sumz[at, :] + b * r.up2[pl.ds(0, n), :]
        if lev == 0:
            used = iota(tot.shape, 1) < ND * HEADS
            inv = 1.0 / jnp.where(used, tot, 1.0)
            a, b = a * inv, b * inv
        r.fa[at, :] = a
        r.fb[at, :] = b


def spread(fac, d):
    hi = fac.astype(bf16)
    lo = (fac - hi.astype(f32)).astype(bf16)
    row = lax.rem(iota((256, D), 0), 128)
    sel = (row == d * HEADS + iota((256, D), 1) // HD).astype(f32).astype(bf16)
    return dot(jnp.concatenate([hi, lo], axis=1), sel)


def up_map(n):
    return (iota((n, n // 2), 0) // 2 == iota((n, n // 2), 1)).astype(f32).astype(bf16)


def combine_values(r):
    for d in range(ND):
        cur = r.num[ext_rows(d, OFF[6], G[6]), :]
        for lev in range(LEVELS - 2, -1, -1):
            n = G[lev]
            low = cur.astype(bf16)
            parts = []
            step = min(n, 128)
            for t in range(n // step):
                at = pl.ds(OFF[lev] + t * step, step)
                own = spread(r.fa[at, :], d) * r.num[ext_rows(d, OFF[lev] + t * step, step), :]
                up = dot(up_map(step), low[t * step // 2 : (t + 1) * step // 2])
                parts.append(own + spread(r.fb[at, :], d) * up)
                if lev == 0:
                    r.ctx[pl.ds(d * LOC + t * step, step), :] = parts[-1].astype(bf16)
            cur = jnp.concatenate(parts, axis=0) if len(parts) > 1 else parts[0]


def attn_out(r):
    def tile(t):
        rows = rows_at(t, RT)
        mid = r.x[rows, :].astype(f32) + dot(r.ctx[rows, :], r.wo[...])
        r.mid[rows, :] = mid
        cen, rstd = stats(mid)
        r.h2[rows, :] = (cen * rstd * r.g2[...] + r.b2[...]).astype(bf16)

    loop(T // RT, tile)


def ffn_inner(r):
    def step(i):
        f, t = i // (T // RT), lax.rem(i, T // RT)
        rows = rows_at(t, RT)
        cols = rows_at(f, 512)
        pre = dot(r.h2[rows, :], r.wup[:, cols])
        ga = dot(r.gy[rows, :], r.wdn[cols, :], 1, 1)
        cdf = 0.5 + 0.5 * lax.erf(pre * (0.5**0.5))
        r.act[rows, cols] = (pre * cdf).astype(bf16)
        pdf = jnp.exp(pre * pre * -0.5) * 0.3989422804014327
        r.gp[rows, cols] = (ga * (cdf + pre * pdf)).astype(bf16)

    loop((FF // 512) * (T // RT), step)


def ffn_grads(r):
    def tile(f):
        cols = rows_at(f, 512)
        r.gdn[cols, :] = dot(r.act[:, cols], r.gy[...], 0, 0).astype(r.gdn.dtype)
        r.gup[:, cols] = dot(r.h2[...], r.gp[:, cols], 0, 0).astype(r.gup.dtype)

    loop(FF // 512, tile)


def norm_back(v, gain, gh, g_gain, g_shift):
    cen, rstd = stats(v)
    xhat = cen * rstd
    g_gain[...] += jnp.sum(gh * xhat, axis=0, keepdims=True)
    g_shift[...] += jnp.sum(gh, axis=0, keepdims=True)
    u = gh * gain
    return rstd * (
        u - jnp.mean(u, axis=-1, keepdims=True) - xhat * jnp.mean(u * xhat, axis=-1, keepdims=True)
    )


def ffn_outer(r):
    r.gg2[...] = jnp.zeros_like(r.gg2)
    r.gb2[...] = jnp.zeros_like(r.gb2)

    def tile(t):
        rows = rows_at(t, RT)
        mid = r.mid[rows, :]
        r.mixed[rows, :] = (mid + dot(r.act[rows, :], r.wdn[...])).astype(bf16)
        gh2 = dot(r.gp[rows, :], r.wup[...], 1, 1)
        g_mid = r.gy[rows, :].astype(f32) + norm_back(mid, r.g2[...], gh2, r.gg2, r.gb2)
        r.gmid[rows, :] = g_mid
        r.gm[rows, :] = g_mid.astype(bf16)

    loop(T // RT, tile)


def out_grads(r):
    r.gwo[...] = dot(r.ctx[...], r.gm[...], 0, 0).astype(r.gwo.dtype)


def attn_back_rows(r):
    lane_head = iota((D, 128), 0) // HD
    for t in range(LOC // 128):
        at = pl.ds(t * 128, 128)
        delta = jnp.zeros((128, 128), f32)
        for d in range(ND):
            rows = pl.ds(d * LOC + t * 128, 128)
            gctx = dot(r.gm[rows, :], r.wo[...], 1, 1)
            sel = (lane_head + d * HEADS == iota((D, 128), 1)).astype(f32).astype(bf16)
            delta = delta + dot((gctx * r.ctx[rows, :].astype(f32)).astype(bf16), sel)
            r.ge[ext_rows(d, t * 128, 128), :] = (spread(r.fa[at, :], d) * gctx).astype(bf16)
            down = (spread(r.fb[at, :], d) * gctx).astype(bf16)
            r.hc[pl.ds(d * LOC // 2 + t * 64, 64), :] = dot(up_map(128), down, 0, 0)
        r.dl[at, :] = (r.fa[at, :] * -delta).astype(bf16)
        r.up[at, :] = r.fb[at, :] * -delta
    acc = r.up[pl.ds(0, LOC // 2, stride=2), :] + r.up[pl.ds(1, LOC // 2, stride=2), :]
    for lev in range(1, LEVELS - 1):
        n = G[lev]
        at = pl.ds(OFF[lev], n)
        r.dl[at, :] = (r.fa[at, :] * acc).astype(bf16)
        r.up[pl.ds(0, n), :] = r.fb[at, :] * acc
        acc = r.up[pl.ds(0, n // 2, stride=2), :] + r.up[pl.ds(1, n // 2, stride=2), :]
    r.dl[pl.ds(OFF[6], 2 * G[6]), :] = jnp.concatenate([acc, jnp.zeros_like(acc)], 0).astype(bf16)
    for d in range(ND):
        cur = r.hc[pl.ds(d * LOC // 2, LOC // 2), :]
        for lev in range(1, LEVELS - 1):
            n = G[lev]
            parts = []
            step = min(n, 128)
            for t in range(n // step):
                at = pl.ds(OFF[lev] + t * step, step)
                seg = cur[t * step : (t + 1) * step]
                own = spread(r.fa[at, :], d) * seg
                r.ge[ext_rows(d, OFF[lev] + t * step, step), :] = own.astype(bf16)
                down = (spread(r.fb[at, :], d) * seg).astype(bf16)
                parts.append(dot(up_map(step), down, 0, 0))
            cur = jnp.concatenate(parts, axis=0) if len(parts) > 1 else parts[0]
        tail = jnp.concatenate([cur, jnp.zeros_like(cur)], axis=0)
        r.ge[ext_rows(d, OFF[6], 2 * G[6]), :] = tail.astype(bf16)


def attend_back_chunk(r, c):
    first = iota((128, 128), 1) < HD
    dl = r.dl[rows_at(c, 128), :]
    for d in range(ND):
        at = pl.ds(pl.multiple_of(d * EXT + c * 128, 128), 128)
        cc = r.cc[at, :]
        for p in range(HEADS // 2):
            lanes = pl.ds(p * 128, 128)
            g = r.ge[at, lanes]
            q = r.qe[at, lanes]
            kcat = split_heads(r.ke[at, lanes])
            vo = jnp.concatenate([split_heads(r.ve[at, lanes]), count_lanes(cc, d, p)], axis=1)
            dp = dot(jnp.concatenate([g, dl], axis=1), vo, 1, 1)
            slot = pl.ds(pl.multiple_of(((c * ND + d) * 4 + p) * 128, 128), 128)
            e = r.wts[slot, :]
            ds = (e.astype(f32) * dp).astype(bf16)
            r.dqe[at, lanes] = dot(ds, kcat).astype(bf16)
            dk = dot(ds, q, 0, 0)
            r.dke[at, lanes] = jnp.where(first, dk[:128], dk[128:]).astype(bf16)
            dv = dot(e, g, 0, 0)
            r.dve[at, lanes] = jnp.where(first, dv[:128], dv[128:]).astype(bf16)


def save_remote(r):
    for d in range(ND):
        r.back[pl.ds(d * 64, 32), :] = r.dke[ext_rows(d, OFF[5], 32), :].astype(f32)
        r.back[pl.ds(d * 64 + 32, 32), :] = r.dve[ext_rows(d, OFF[5], 32), :].astype(f32)


def unpool_levels(r, z):
    keep = OFF[5] - LOC
    zeros = jnp.zeros((LOC - keep - 24, D), f32)
    for d in range(ND):
        inv, inv_size = inv_counts(r, z, d)
        fine = ext_rows(d, 0, LOC)
        rows = pl.ds(d * LOC, LOC)
        live = live_rows(r, z, d, 0, LOC)
        q = (r.dqe[ext_rows(d, LOC, LOC), :].astype(f32) * wide(inv_size)).astype(bf16)
        q = r.dqe[fine, :].astype(f32) + dot(r.unpool[...], q)
        r.gqkv[rows, 0:D] = (q * (HD**-0.5)).astype(bf16)
        own = r.dke[ext_rows(d, LOC, keep), :].astype(f32)
        k = jnp.concatenate([own, r.cg[pl.ds(d * 48, 24), :], zeros], axis=0)
        k = (k * wide(inv)).astype(bf16)
        k = r.dke[fine, :].astype(f32) + dot(r.unpool[...], k)
        r.gqkv[rows, D : 2 * D] = jnp.where(live, k, 0.0).astype(bf16)
        own = r.dve[ext_rows(d, LOC, keep), :].astype(f32)
        v = jnp.concatenate([own, r.cg[pl.ds(d * 48 + 24, 24), :], zeros], axis=0).astype(bf16)
        v = r.dve[fine, :].astype(f32) + dot(r.unpool[...], v)
        r.gqkv[rows, 2 * D : 3 * D] = jnp.where(live, v, 0.0).astype(bf16)


def qkv_grads(r):
    def tile(i):
        cols = rows_at(i, 512)
        r.gwqkv[:, cols] = dot(r.h1[...], r.gqkv[:, cols], 0, 0).astype(r.gwqkv.dtype)

    loop(3, tile)


def input_grads(r):
    r.gg1[...] = jnp.zeros_like(r.gg1)
    r.gb1[...] = jnp.zeros_like(r.gb1)

    def tile(t):
        rows = rows_at(t, RT)
        gh1 = dot(r.gqkv[rows, :], r.wqkv[...], 1, 1)
        x = r.x[rows, :].astype(f32)
        r.gx[rows, :] = r.gmid[rows, :] + norm_back(x, r.g1[...], gh1, r.gg1, r.gb1)

    loop(T // RT, tile)


def first_kernel(r):
    z = lax.axis_index("mp")
    build_maps(r)
    norm_one(r)
    project(r, z)
    pool_levels(r, z)


def second_kernel(r):
    z = lax.axis_index("mp")
    build_tables(r, z)
    loop(EXT // 128, lambda c: attend_chunk(r, c))
    combine_sums(r)
    combine_values(r)
    attn_out(r)
    ffn_inner(r)
    ffn_grads(r)
    ffn_outer(r)
    out_grads(r)
    attn_back_rows(r)
    loop(EXT // 128, lambda c: attend_back_chunk(r, c))
    save_remote(r)


def third_kernel(r):
    z = lax.axis_index("mp")
    build_maps(r)
    unpool_levels(r, z)
    qkv_grads(r)
    input_grads(r)


def run(body, ins, outs, scratch):
    names = list(ins) + list(outs) + list(scratch)

    def kernel(*refs):
        body(types.SimpleNamespace(**dict(zip(names, refs))))

    vmem = pl.BlockSpec(memory_space=pltpu.VMEM)
    smem = pl.BlockSpec(memory_space=pltpu.SMEM)
    result = pl.pallas_call(
        kernel,
        out_shape=[jax.ShapeDtypeStruct(*v) for v in outs.values()],
        in_specs=[smem if n == "lens" else vmem for n in ins],
        out_specs=[vmem] * len(outs),
        scratch_shapes=[pltpu.VMEM(*v) for v in scratch.values()],
        compiler_params=pltpu.CompilerParams(vmem_limit_bytes=60 * 1024 * 1024),
    )(*ins.values())
    return dict(zip(outs, result))


def gather_columns(w):
    full = lax.all_gather(w, "mp", axis=0)
    return jnp.moveaxis(full, 0, 1).reshape(w.shape[0], -1)


def per_device(
    tokens,
    lengths,
    gain_one,
    shift_one,
    w_query,
    w_key,
    w_value,
    w_output,
    gain_two,
    shift_two,
    w_up,
    w_down,
    cotangent,
):
    z = lax.axis_index("mp")
    x = jnp.swapaxes(tokens, 0, 1).reshape(T, D)
    gy = jnp.swapaxes(cotangent, 0, 1).reshape(T, D)
    g1, b1, g2, b2 = (v.reshape(1, D) for v in (gain_one, shift_one, gain_two, shift_two))
    wqkv = jnp.concatenate([gather_columns(w) for w in (w_query, w_key, w_value)], axis=1)
    wo = lax.all_gather(w_output, "mp", axis=0, tiled=True)
    wup = gather_columns(w_up)
    wdn = lax.all_gather(w_down, "mp", axis=0, tiled=True)
    one = run(
        first_kernel,
        dict(lens=lengths, x=x, g1=g1, b1=b1, wqkv=wqkv),
        dict(
            h1=((T, D), bf16),
            qe=((ND * EXT, D), bf16),
            ke=((ND * EXT, D), bf16),
            ve=((ND * EXT, D), bf16),
            sums=((ND * 48, D), f32),
        ),
        dict(pool=((EXT - LOC, LOC), bf16), unpool=((LOC, EXT - LOC), bf16)),
    )
    everyone = lax.all_gather(one["sums"].reshape(ND, 2, 24, D), "mp", axis=0)
    near = z + 1 - 2 * (z % 2)
    far = (1 - z // 2) * 2

    def pick(i):
        return lax.dynamic_index_in_dim(everyone, i, 0, keepdims=False)

    rem = jnp.concatenate(
        [pick(near)[:, :, :16], pick(far)[:, :, 16:], pick(far + 1)[:, :, 16:]], axis=2
    )
    rem3 = rem.astype(bf16)
    ke = one["ke"].reshape(ND, EXT, D).at[:, OFF[5] :].set(rem3[:, 0]).reshape(ND * EXT, D)
    ve = one["ve"].reshape(ND, EXT, D).at[:, OFF[5] :].set(rem3[:, 1]).reshape(ND * EXT, D)
    two = run(
        second_kernel,
        dict(
            lens=lengths, x=x, gy=gy, g2=g2, b2=b2, qe=one["qe"], ke=ke, ve=ve,
            wo=wo, wup=wup, wdn=wdn,
        ),
        dict(
            mixed=((T, D), bf16),
            gmid=((T, D), f32),
            dqe=((ND * EXT, D), bf16),
            dke=((ND * EXT, D), bf16),
            dve=((ND * EXT, D), bf16),
            back=((ND * 64, D), f32),
            gwo=((D, D), bf16),
            gup=((D, FF), bf16),
            gdn=((FF, D), bf16),
            gg2=((1, D), f32),
            gb2=((1, D), f32),
        ),
        dict(
            cc=((ND * EXT, 128), bf16),
            bias=((ND * EXT, 128), f32),
            wts=((64 * 128, 256), bf16),
            num=((ND * EXT, D), f32),
            tops=((EXT, 128), f32),
            sumz=((EXT, 128), f32),
            up=((LOC, 128), f32),
            up2=((LOC, 128), f32),
            fa=((EXT, 128), f32),
            fb=((EXT, 128), f32),
            ctx=((T, D), bf16),
            mid=((T, D), f32),
            h2=((T, D), bf16),
            act=((T, FF), bf16),
            gp=((T, FF), bf16),
            gm=((T, D), bf16),
            ge=((ND * EXT, D), bf16),
            hc=((T // 2, D), f32),
            dl=((EXT, 128), bf16),
        ),
    )
    backs = lax.all_gather(two["back"].reshape(ND, 2, 32, D), "mp", axis=0)

    def pick_back(i, first, count):
        return lax.dynamic_index_in_dim(backs, i, 0, keepdims=False)[:, :, first : first + count]

    mine = z % 2
    from_far = [
        jnp.where(mine == 0, pick_back(far + j, 16, 8), pick_back(far + j, 24, 8)) for j in range(2)
    ]
    cg = jnp.concatenate([pick_back(near, 0, 16), from_far[0] + from_far[1]], axis=2)
    three = run(
        third_kernel,
        dict(
            lens=lengths, x=x, g1=g1, b1=b1, h1=one["h1"], wqkv=wqkv, gmid=two["gmid"],
            dqe=two["dqe"], dke=two["dke"], dve=two["dve"], cg=cg.reshape(ND * 48, D),
        ),
        dict(
            gx=((T, D), f32),
            gwqkv=((D, 3 * D), bf16),
            gg1=((1, D), f32),
            gb1=((1, D), f32),
        ),
        dict(
            pool=((EXT - LOC, LOC), bf16),
            unpool=((LOC, EXT - LOC), bf16),
            gqkv=((T, 3 * D), bf16),
        ),
    )

    def scatter(g, axis):
        part = lax.psum_scatter(g, "mp", scatter_dimension=axis, tiled=True)
        return lax.psum(part, "dp").astype(f32)

    gw = three["gwqkv"]
    norms = lax.psum((three["gg1"], three["gb1"], two["gg2"], two["gb2"]), ("dp", "mp"))

    def back_to(a):
        return jnp.swapaxes(a.reshape(ND, LOC, D), 0, 1)

    return (
        back_to(two["mixed"]),
        back_to(three["gx"]),
        scatter(gw[:, :D], 1),
        scatter(gw[:, D : 2 * D], 1),
        scatter(gw[:, 2 * D :], 1),
        scatter(two["gwo"], 0),
        scatter(two["gup"], 1),
        scatter(two["gdn"], 0),
        *(v.reshape(D) for v in norms),
    )


def solution(mesh):
    tok = P("mp", "dp", None)
    col, row, rep = P(None, "mp"), P("mp", None), P()
    return jax.shard_map(
        per_device,
        mesh=mesh,
        in_specs=(tok, P("dp"), rep, rep, col, col, col, row, rep, rep, col, row, tok),
        out_specs=(tok, tok, col, col, col, row, col, row, rep, rep, rep, rep),
        check_vma=False,
    )
```

```python
import types

import jax
import jax.numpy as jnp
from jax import lax
from jax.experimental import pallas as pl
from jax.experimental.pallas import tpu as pltpu
from jax.sharding import PartitionSpec as P

HD = 64
BLK = 16
NEG = -1e30
FLOOR = -1e29
EPS = 1e-05
LOC = 512
ND = 2
D = 512
FF = 2048
NMP = 4
HALF = 256
T = ND * LOC
HEADS = D // HD
LEVELS = 7
LOCAL_LEVELS = 5
EXT = 1024
RT = 256
G = [LOC >> lev for lev in range(LEVELS)]
OFF = [sum(G[:lev]) for lev in range(LEVELS)]
bf16 = jnp.bfloat16
f32 = jnp.float32
i32 = jnp.int32


def dot(a, b, ca=1, cb=0):
    return lax.dot_general(a, b, (((ca,), (cb,)), ((), ())), preferred_element_type=f32)


def iota(shape, axis):
    return lax.broadcasted_iota(i32, shape, axis)


def loop(n, body):
    lax.fori_loop(0, n, lambda i, c: (body(i), c)[1], 0)


def rows_at(i, size):
    return pl.ds(pl.multiple_of(i * size, size), size)


def own_groups(e):
    size = jnp.zeros_like(e)
    start = jnp.zeros_like(e)
    for lev in range(LEVELS):
        here = (e >= OFF[lev]) & (e < OFF[lev] + G[lev])
        size = jnp.where(here, 1 << lev, size)
        start = jnp.where(here, (e - OFF[lev]) << lev, start)
    return size, start


def key_groups(e, z):
    size, start = own_groups(e)
    start = start + z * LOC
    near = z + 1 - 2 * lax.rem(z, 2)
    far = 1 - z // 2
    size = jnp.where(e >= OFF[5], 32, size)
    start = jnp.where(e >= OFF[5], near * LOC + (e - OFF[5]) * 32, start)
    size = jnp.where(e >= OFF[6], 64, size)
    start = jnp.where(e >= OFF[6], far * 2 * LOC + (e - OFF[6]) * 64, start)
    return size, start


def count_live(size, start, length):
    return jnp.clip(length - start, 0, size).astype(f32)


def build_tables(r, z):
    for d in range(ND):
        r.ee[d] = head_map(d)
        length = r.lens[d]

        def chunk(c, d=d, length=length):
            at = pl.ds(pl.multiple_of(d * EXT + c * 128, 128), 128)
            e_col = iota((128, 128), 0) + c * 128
            size, start = key_groups(e_col, z)
            r.cc[at, :] = count_live(size, start, length).astype(bf16)
            e_row = iota((1, 128), 1) + c * 128
            size, start = key_groups(e_row, z)
            dead = count_live(size, start, length)
            r.crow[pl.ds(d * (EXT // 128) + c, 1), :] = dead
            q_blk, k_blk = e_col // BLK, jnp.broadcast_to(e_row // BLK, (128, 128))
            span = jnp.where(q_blk // 2 == k_blk // 2, 0.0, NEG)
            same = jnp.where(q_blk == k_blk, 0.0, NEG)
            cross = jnp.where(q_blk == k_blk, NEG, span)
            bias = jnp.where(e_col < LOC, span, jnp.where(e_col < OFF[5], cross, same))
            r.bias[at, :] = jnp.where(jnp.broadcast_to(dead, (128, 128)) > 0.0, bias, NEG)

        loop(EXT // 128, chunk)


def build_maps(r):
    def tile(c):
        rows = rows_at(c, 128)
        size, start = own_groups(iota((128, LOC), 0) + c * 128 + LOC)
        pos = iota((128, LOC), 1)
        r.pool[rows, :] = ((pos >= start) & (pos < start + size)).astype(f32).astype(bf16)
        size, start = own_groups(iota((128, EXT - LOC), 1) + LOC)
        pos = iota((128, EXT - LOC), 0) + c * 128
        r.unpool[rows, :] = ((pos >= start) & (pos < start + size)).astype(f32).astype(bf16)

    loop((EXT - LOC) // 128, tile)


def inv_counts(r, z, d):
    e = iota((EXT - LOC, 128), 0) + LOC
    size, start = own_groups(e)
    cnt = count_live(size, start + z * LOC, r.lens[d])
    return 1.0 / jnp.maximum(cnt, 1.0), 1.0 / jnp.maximum(size, 1).astype(f32)


def wide(col):
    return jnp.concatenate([col] * (D // 128), axis=1)


def live_rows(r, z, d, first, count):
    pos = iota((count, D), 0) + first + z * LOC
    return pos < r.lens[d]


def stats(v):
    mean = jnp.mean(v, axis=-1, keepdims=True)
    cen = v - mean
    var = jnp.mean(cen * cen, axis=-1, keepdims=True)
    return cen, lax.rsqrt(var + EPS)


def norm_one(r):
    def tile(t):
        rows = rows_at(t, RT)
        cen, rstd = stats(r.x[rows, :].astype(f32))
        r.h1[rows, :] = (cen * rstd * r.g1[...] + r.b1[...]).astype(bf16)

    loop(T // RT, tile)


def ext_rows(d, off, count):
    return pl.ds(d * EXT + off, count)


def attn_weight(r, t):
    return jnp.concatenate([r.wat[s, :, t * 128 : (t + 1) * 128] for s in range(NMP)], axis=1)


def project(r, z, d):
    def tile(t):
        rows = pl.ds(pl.multiple_of(d * LOC + t * RT, RT), RT)
        at = pl.ds(pl.multiple_of(d * EXT + t * RT, RT), RT)
        h = r.h1[rows, :]
        live = live_rows(r, z, d, t * RT, RT)
        q = dot(h, attn_weight(r, 0)).astype(bf16).astype(f32)
        r.qe[at, :] = (q * (HD**-0.5)).astype(bf16)
        k = dot(h, attn_weight(r, 1))
        r.ke[at, :] = jnp.where(live, k, 0.0).astype(bf16)
        v = dot(h, attn_weight(r, 2))
        r.ve[at, :] = jnp.where(live, v, 0.0).astype(bf16)

    loop(LOC // RT, tile)


def pool_levels(r, z):
    keep = OFF[5] - LOC
    for d in range(ND):
        inv, inv_size = inv_counts(r, z, d)
        fine = ext_rows(d, 0, LOC)
        coarse = ext_rows(d, LOC, LOC)
        r.qe[coarse, :] = (dot(r.pool[...], r.qe[fine, :]) * wide(inv_size)).astype(bf16)
        k = dot(r.pool[...], r.ke[fine, :]) * wide(inv)
        v = dot(r.pool[...], r.ve[fine, :])
        r.ke[ext_rows(d, LOC, keep), :] = k[:keep].astype(bf16)
        r.ve[ext_rows(d, LOC, keep), :] = v[:keep].astype(bf16)
        r.sums[2 * d] = k[keep : keep + 24]
        r.sums[2 * d + 1] = v[keep : keep + 24]


def place_remote(r):
    for d in range(ND):
        r.ke[ext_rows(d, OFF[5], 32), :] = r.rem[2 * d].astype(bf16)
        r.ve[ext_rows(d, OFF[5], 32), :] = r.rem[2 * d + 1].astype(bf16)


def split_heads(pair):
    first = iota(pair.shape, 1) < HD
    zero = jnp.zeros_like(pair)
    return jnp.concatenate([jnp.where(first, pair, zero), jnp.where(first, zero, pair)], axis=0)


def count_lanes(cc, d, p):
    lane = iota(cc.shape, 1)
    zero = jnp.zeros_like(cc)
    a = jnp.where(lane == d * HEADS + 2 * p, cc, zero)
    b = jnp.where(lane == d * HEADS + 2 * p + 1, cc, zero)
    return jnp.concatenate([a, b], axis=0)


def attend_chunk(r, c):
    lane = iota((128, 128), 1)
    tops = jnp.zeros((128, 128), f32)
    sums = jnp.zeros((128, 128), f32)
    for d in range(ND):
        at = pl.ds(pl.multiple_of(d * EXT + c * 128, 128), 128)
        bias = r.bias[at, :]
        cc = r.cc[at, :]
        for p in range(HEADS // 2):
            lanes = pl.ds(p * 128, 128)
            s = dot(r.qe[at, lanes], split_heads(r.ke[at, lanes]), 1, 1)
            parts = []
            for j in range(2):
                sj = s[:, j * 128 : (j + 1) * 128] + bias
                top = jnp.maximum(jnp.max(sj, axis=1, keepdims=True), FLOOR)
                parts.append(jnp.exp(sj - top))
                tops = jnp.where(lane == d * HEADS + 2 * p + j, top, tops)
            e = jnp.concatenate(parts, axis=1).astype(bf16)
            slot = pl.ds(pl.multiple_of(((c * ND + d) * 4 + p) * 128, 128), 128)
            r.wts[slot, :] = e
            vo = jnp.concatenate([split_heads(r.ve[at, lanes]), count_lanes(cc, d, p)], axis=1)
            o = dot(e, vo)
            r.num[at, lanes] = o[:, :128]
            sums = sums + o[:, 128:]
    here = rows_at(c, 128)
    r.tops[here, :] = tops
    r.sumz[here, :] = sums


def combine_sums(r):
    last = pl.ds(OFF[6], G[6])
    top = r.tops[last, :]
    tot = r.sumz[last, :]
    for lev in range(LEVELS - 2, -1, -1):
        n = G[lev]
        for half in range(2):
            r.up[pl.ds(half, n // 2, stride=2), :] = top
            r.up2[pl.ds(half, n // 2, stride=2), :] = tot
        at = pl.ds(OFF[lev], n)
        up_top = r.up[pl.ds(0, n), :]
        own = r.tops[at, :]
        top = jnp.maximum(own, up_top)
        a = jnp.exp(own - top)
        b = jnp.exp(up_top - top)
        tot = a * r.sumz[at, :] + b * r.up2[pl.ds(0, n), :]
        if lev == 0:
            used = iota(tot.shape, 1) < ND * HEADS
            inv = 1.0 / jnp.where(used, tot, 1.0)
            a, b = a * inv, b * inv
        r.fa[at, :] = a
        r.fb[at, :] = b


def high_low(v, axis):
    hi = v.astype(bf16).astype(f32)
    return jnp.concatenate([hi, v - hi], axis=axis).astype(bf16)


def spread(r, fac, d):
    return dot(high_low(fac, 1), r.ee[d])


def head_map(d):
    row = lax.rem(iota((256, D), 0), 128)
    return (row == d * HEADS + iota((256, D), 1) // HD).astype(f32).astype(bf16)


def up_map(n):
    return (iota((n, n), 0) // 2 == lax.rem(iota((n, n), 1), n // 2)).astype(f32).astype(bf16)


def down_map(n):
    return (lax.rem(iota((2 * n, n // 2), 0), n) // 2 == iota((2 * n, n // 2), 1)).astype(f32).astype(bf16)


def combine_values(r):
    for d in range(ND):
        cur = r.num[ext_rows(d, OFF[6], G[6]), :]
        for lev in range(LEVELS - 2, -1, -1):
            n = G[lev]
            parts = []
            step = min(n, 128)
            for t in range(n // step):
                at = pl.ds(OFF[lev] + t * step, step)
                here = ext_rows(d, OFF[lev] + t * step, step)
                own = spread(r, r.fa[at, :], d) * r.num[here, :]
                up = dot(up_map(step), high_low(cur[t * step // 2 : (t + 1) * step // 2], 0))
                parts.append(own + spread(r, r.fb[at, :], d) * up)
                if lev == 0:
                    r.ctx[pl.ds(d * LOC + t * step, step), :] = parts[-1].astype(bf16)
                    r.num[here, :] = parts[-1]
            cur = jnp.concatenate(parts, axis=0) if len(parts) > 1 else parts[0]


def spare_rows(t):
    per = LOC // RT
    return pl.ds(pl.multiple_of((t // per) * EXT + LOC + lax.rem(t, per) * RT, RT), RT)


def attn_out(r):
    def tile(t):
        rows = rows_at(t, RT)
        mid = r.x[rows, :].astype(f32) + dot(r.ctx[rows, :], attn_weight(r, 3), 1, 1)
        r.num[spare_rows(t), :] = mid
        cen, rstd = stats(mid)
        r.h2[rows, :] = (cen * rstd * r.g2[...] + r.b2[...]).astype(bf16)

    loop(T // RT, tile)


def ffn_inner(r):
    def step(i):
        f, t = i // (T // RT), lax.rem(i, T // RT)
        rows = rows_at(t, RT)
        cols = rows_at(f, 512)
        pre = dot(r.h2[rows, :], r.wup[f])
        ga = dot(r.gy[rows, :], r.wdn[f], 1, 1)
        cdf = 0.5 + 0.5 * lax.erf(pre * (0.5**0.5))
        r.act[rows, cols] = (pre * cdf).astype(bf16)
        pdf = jnp.exp(pre * pre * -0.5) * 0.3989422804014327
        r.gp[rows, cols] = (ga * (cdf + pre * pdf)).astype(bf16)

    loop((FF // 512) * (T // RT), step)


def down_grads(r):
    def tile(f):
        r.gdn[f] = dot(r.act[:, rows_at(f, 512)], r.gy[...], 0, 0).astype(bf16)

    loop(NMP, tile)


def up_grads(r):
    def tile(f):
        r.gup[f] = dot(r.h2[...], r.gp[:, rows_at(f, 512)], 0, 0).astype(bf16)

    loop(NMP, tile)


def norm_back(v, gain, gh, r, row):
    cen, rstd = stats(v)
    xhat = cen * rstd
    r.norms[row : row + 1, :] += jnp.sum(gh * xhat, axis=0, keepdims=True)
    r.norms[row + 1 : row + 2, :] += jnp.sum(gh, axis=0, keepdims=True)
    u = gh * gain
    return rstd * (
        u - jnp.mean(u, axis=-1, keepdims=True) - xhat * jnp.mean(u * xhat, axis=-1, keepdims=True)
    )


def ffn_outer(r):
    def tile(t):
        rows = rows_at(t, RT)
        mid = r.num[spare_rows(t), :]
        ffn = dot(r.act[rows, 0:512], r.wdn[0])
        gh2 = dot(r.gp[rows, 0:512], r.wup[0], 1, 1)
        for f in range(1, NMP):
            cols = slice(f * 512, (f + 1) * 512)
            ffn = ffn + dot(r.act[rows, cols], r.wdn[f])
            gh2 = gh2 + dot(r.gp[rows, cols], r.wup[f], 1, 1)
        r.mixed[rows, :] = (mid + ffn).astype(bf16)
        g_mid = r.gy[rows, :].astype(f32) + norm_back(mid, r.g2[...], gh2, r, 2)
        r.gx[rows, :] = g_mid
        r.gm[rows, :] = g_mid.astype(bf16)

    loop(T // RT, tile)


def store_shards(dst, full):
    for s in range(NMP):
        dst[s] = full[:, s * 128 : (s + 1) * 128].astype(bf16)


def out_grads(r):
    store_shards(r.gw3, dot(r.gm[...], r.ctx[...], 0, 0))


def store_pair(r, d, off, count, v):
    hi = v.astype(bf16)
    r.ge[ext_rows(d, off, count), :] = hi
    lo = (v - hi.astype(f32)).astype(bf16)
    if off < LOC:
        r.dqe[ext_rows(d, off, count), :] = lo
    else:
        r.dke[ext_rows(d, off - LOC, count), :] = lo


def attn_back_rows(r):
    lane_head = lax.rem(iota((2 * D, 128), 0), D) // HD
    for t in range(LOC // 128):
        at = pl.ds(t * 128, 128)
        delta = jnp.zeros((128, 128), f32)
        for d in range(ND):
            rows = pl.ds(d * LOC + t * 128, 128)
            gctx = dot(r.gm[rows, :], attn_weight(r, 3))
            sel = (lane_head + d * HEADS == iota((2 * D, 128), 1)).astype(f32).astype(bf16)
            delta = delta + dot(high_low(gctx * r.num[ext_rows(d, t * 128, 128), :], 1), sel)
            store_pair(r, d, t * 128, 128, spread(r, r.fa[at, :], d) * gctx)
            down = high_low(spread(r, r.fb[at, :], d) * gctx, 0)
            r.hc[pl.ds(d * LOC // 2 + t * 64, 64), :] = dot(down_map(128), down, 0, 0)
        r.dl[at, :] = r.fa[at, :] * delta
        r.up[at, :] = r.fb[at, :] * delta
    acc = r.up[pl.ds(0, LOC // 2, stride=2), :] + r.up[pl.ds(1, LOC // 2, stride=2), :]
    for lev in range(1, LEVELS - 1):
        n = G[lev]
        at = pl.ds(OFF[lev], n)
        r.dl[at, :] = r.fa[at, :] * acc
        r.up[pl.ds(0, n), :] = r.fb[at, :] * acc
        acc = r.up[pl.ds(0, n // 2, stride=2), :] + r.up[pl.ds(1, n // 2, stride=2), :]
    r.dl[pl.ds(OFF[6], 2 * G[6]), :] = jnp.concatenate([acc, jnp.zeros_like(acc)], 0)
    for d in range(ND):
        cur = r.hc[pl.ds(d * LOC // 2, LOC // 2), :]
        for lev in range(1, LEVELS - 1):
            n = G[lev]
            parts = []
            step = min(n, 128)
            for t in range(n // step):
                at = pl.ds(OFF[lev] + t * step, step)
                seg = cur[t * step : (t + 1) * step]
                store_pair(r, d, OFF[lev] + t * step, step, spread(r, r.fa[at, :], d) * seg)
                down = high_low(spread(r, r.fb[at, :], d) * seg, 0)
                parts.append(dot(down_map(step), down, 0, 0))
            cur = jnp.concatenate(parts, axis=0) if len(parts) > 1 else parts[0]
        store_pair(r, d, OFF[6], 2 * G[6], jnp.concatenate([cur, jnp.zeros_like(cur)], axis=0))


def attend_back_chunk(r, c, fine):
    first = iota((128, 128), 1) < HD
    dl = r.dl[rows_at(c, 128), :]
    low = r.dqe if fine else r.dke
    for d in range(ND):
        at = pl.ds(pl.multiple_of(d * EXT + c * 128, 128), 128)
        low_at = at if fine else pl.ds(pl.multiple_of(d * EXT + c * 128 - LOC, 128), 128)
        cnt = jnp.broadcast_to(r.crow[pl.ds(d * (EXT // 128) + c, 1), :], (128, 128))
        for p in range(HEADS // 2):
            lanes = pl.ds(p * 128, 128)
            g = r.ge[at, lanes]
            q = r.qe[at, lanes]
            kcat = split_heads(r.ke[at, lanes])
            vcat = split_heads(r.ve[at, lanes])
            both = jnp.concatenate([g, low[low_at, lanes]], axis=1)
            dp = dot(both, jnp.concatenate([vcat, vcat], axis=1), 1, 1)
            slot = pl.ds(pl.multiple_of(((c * ND + d) * 4 + p) * 128, 128), 128)
            e = r.wts[slot, :]
            parts = []
            for j in range(2):
                lane = d * HEADS + 2 * p + j
                half = slice(j * 128, (j + 1) * 128)
                parts.append(e[:, half].astype(f32) * (dp[:, half] - dl[:, lane : lane + 1] * cnt))
            ds = jnp.concatenate(parts, axis=1).astype(bf16)
            dq = dot(ds, kcat)
            dk = dot(ds, q, 0, 0)
            dk = jnp.where(first, dk[:128], dk[128:])
            if fine:
                r.num[pl.ds(pl.multiple_of(d * EXT + c * 128, 128), 128), lanes] = dq
                r.num[pl.ds(pl.multiple_of(d * EXT + LOC + c * 128, 128), 128), lanes] = dk
            else:
                r.dqe[at, lanes] = dq.astype(bf16)
                r.dke[at, lanes] = dk.astype(bf16)
            dv = dot(e, g, 0, 0)
            r.dve[at, lanes] = jnp.where(first, dv[:128], dv[128:]).astype(bf16)


def save_remote(r):
    for d in range(ND):
        r.back[2 * d] = r.dke[ext_rows(d, OFF[5], 32), :].astype(f32)
        r.back[2 * d + 1] = r.dve[ext_rows(d, OFF[5], 32), :].astype(f32)


def coarse_rows(r, src, d, kv):
    keep = OFF[5] - LOC
    own = src[ext_rows(d, LOC, keep), :].astype(f32)
    i = 2 * d + kv
    rest = jnp.zeros((LOC - keep - 24, D), f32)
    return jnp.concatenate([own, r.near[i], r.far[0, i] + r.far[1, i], rest], axis=0)


def unpool_values(r, z):
    for d in range(ND):
        live = live_rows(r, z, d, 0, LOC)
        v = coarse_rows(r, r.dve, d, 1).astype(bf16)
        v = r.dve[ext_rows(d, 0, LOC), :].astype(f32) + dot(r.unpool[...], v)
        r.ve[pl.ds(d * LOC, LOC), :] = jnp.where(live, v, 0.0).astype(bf16)


def unpool_keys(r, z):
    for d in range(ND):
        inv, _ = inv_counts(r, z, d)
        live = live_rows(r, z, d, 0, LOC)
        k = (coarse_rows(r, r.dke, d, 0) * wide(inv)).astype(bf16)
        k = r.num[ext_rows(d, LOC, LOC), :] + dot(r.unpool[...], k)
        r.ke[pl.ds(d * LOC, LOC), :] = jnp.where(live, k, 0.0).astype(bf16)


def unpool_queries(r, z):
    for d in range(ND):
        _, inv_size = inv_counts(r, z, d)
        q = (r.dqe[ext_rows(d, LOC, LOC), :].astype(f32) * wide(inv_size)).astype(bf16)
        q = r.num[ext_rows(d, 0, LOC), :] + dot(r.unpool[...], q)
        r.qe[pl.ds(d * LOC, LOC), :] = (q * (HD**-0.5)).astype(bf16)


def weight_grad(r, dst, src):
    store_shards(dst, dot(r.h1[...], src[pl.ds(0, T), :], 0, 0))


def input_grads(r, t):
    rows = rows_at(t, RT)
    gh1 = dot(r.qe[rows, :], attn_weight(r, 0), 1, 1)
    gh1 = gh1 + dot(r.ke[rows, :], attn_weight(r, 1), 1, 1)
    gh1 = gh1 + dot(r.ve[rows, :], attn_weight(r, 2), 1, 1)
    x = r.x[rows, :].astype(f32)
    r.gx[rows, :] = r.gx[rows, :] + norm_back(x, r.g1[...], gh1, r, 0)


def remote(src, dst, send, recv, where):
    return pltpu.make_async_remote_copy(
        src_ref=src, dst_ref=dst, send_sem=send, recv_sem=recv, device_id=where,
        device_id_type=pl.DeviceIdType.MESH,
    )


class Links:
    def __init__(self, r, ndp):
        self.r, self.ndp, self.nq, self.piece = r, ndp, ndp // 2, LOC // ndp
        self.z, self.me = lax.axis_index("mp"), lax.axis_index("dp")
        self.c, self.q = lax.rem(self.me, 2), self.me // 2
        self.other = 2 * self.q + 1 - self.c
        self.near = self.z + 1 - 2 * lax.rem(self.z, 2)
        self.far = (1 - self.z // 2) * 2
        self.par = lax.rem(self.z, 2)
        self.sent = []

    def mp_peer(self, k):
        return lax.rem(self.z + k, NMP)

    def dp_peer(self, k):
        return lax.rem(self.me + k, self.ndp)

    def quarter(self, j):
        return lax.rem(self.q + j, self.nq)

    def piece_rows(self, q):
        return pl.ds(pl.multiple_of(self.c * HALF + q * self.piece, self.piece), self.piece)

    def rows_of(self, dev):
        first = lax.rem(dev, 2) * HALF + (dev // 2) * self.piece
        return pl.ds(pl.multiple_of(first, self.piece), self.piece)

    def half(self, c):
        return pl.ds(pl.multiple_of(c * HALF, HALF), HALF)

    def send(self, src, dst, send, recv, where):
        copy = remote(src, dst, send, recv, where)
        copy.start()
        self.sent.append(copy)

    def arrive(self, dst, send, recv, where):
        remote(dst, dst, send, recv, where).wait_recv()

    def barrier(self):
        sem = pltpu.get_barrier_semaphore()
        for k in range(1, NMP):
            pl.semaphore_signal(sem, inc=1, device_id={"mp": self.mp_peer(k)})
        for k in range(1, self.ndp):
            pl.semaphore_signal(sem, inc=1, device_id={"dp": self.dp_peer(k)})
        pl.semaphore_wait(sem, NMP + self.ndp - 2)

    def gather_z(self, m, w):
        rows = self.rows_of(self.me)
        for k in range(1, NMP):
            piece = w.at[self.z, rows, :]
            i = m * 3 + k - 1
            self.send(piece, piece, self.r.wz_s.at[i], self.r.wz_r.at[i], {"mp": self.mp_peer(k)})

    def gather_plane(self, m, w):
        rows = self.rows_of(self.me)
        for k in range(1, NMP):
            piece = w.at[self.mp_peer(NMP - k), rows, :]
            i = m * 3 + k - 1
            here = {"mp": self.mp_peer(k)}
            self.arrive(piece, self.r.wz_s.at[i], self.r.wz_r.at[i], here)
            for j in range(1, self.nq):
                n = i * (self.nq - 1) + j - 1
                where = {"dp": 2 * self.quarter(j) + self.c}
                self.send(piece, piece, self.r.wp_s.at[n], self.r.wp_r.at[n], where)

    def gather_core(self, m, w):
        for k in range(1, NMP):
            shard = self.mp_peer(NMP - k)
            i = m * 3 + k - 1
            for j in range(1, self.nq):
                n = i * (self.nq - 1) + j - 1
                got = w.at[shard, self.piece_rows(self.quarter(self.nq - j)), :]
                where = {"dp": 2 * self.quarter(j) + self.c}
                self.arrive(got, self.r.wp_s.at[n], self.r.wp_r.at[n], where)
            part = w.at[shard, self.half(self.c), :]
            self.send(part, part, self.r.wc_s.at[i], self.r.wc_r.at[i], {"dp": self.other})

    def gather_done(self, m, w):
        for k in range(1, NMP):
            i = m * 3 + k - 1
            part = w.at[self.mp_peer(NMP - k), self.half(1 - self.c), :]
            self.arrive(part, self.r.wc_s.at[i], self.r.wc_r.at[i], {"dp": self.other})

    def coarse_send(self):
        r = self.r
        dst = r.rem.at[:, pl.ds(0, 16), :]
        self.send(r.sums.at[:, pl.ds(0, 16), :], dst, r.cf_s.at[0], r.cf_r.at[0], {"mp": self.near})
        place = pl.ds(pl.multiple_of(16 + 8 * self.par, 8), 8)
        for j in range(2):
            where = {"mp": self.far + j}
            src = r.sums.at[:, pl.ds(16, 8), :]
            dst = r.rem.at[:, place, :]
            self.send(src, dst, r.cf_s.at[1 + j], r.cf_r.at[1 + self.par], where)

    def coarse_wait(self):
        r = self.r
        self.arrive(r.rem.at[:, pl.ds(0, 16), :], r.cf_s.at[0], r.cf_r.at[0], {"mp": self.near})
        for j in range(2):
            got = r.rem.at[:, pl.ds(16 + 8 * j, 8), :]
            self.arrive(got, r.cf_s.at[1 + j], r.cf_r.at[1 + j], {"mp": self.far + j})

    def coarse_back(self):
        r = self.r
        src = r.back.at[:, pl.ds(0, 16), :]
        self.send(src, r.near, r.cb_s.at[0], r.cb_r.at[0], {"mp": self.near})
        for j in range(2):
            src = r.back.at[:, pl.ds(16 + 8 * j, 8), :]
            dst = r.far.at[self.par]
            self.send(src, dst, r.cb_s.at[1 + j], r.cb_r.at[1 + self.par], {"mp": self.far + j})

    def coarse_back_wait(self):
        r = self.r
        self.arrive(r.near, r.cb_s.at[0], r.cb_r.at[0], {"mp": self.near})
        for j in range(2):
            self.arrive(r.far.at[j], r.cb_s.at[1 + j], r.cb_r.at[1 + j], {"mp": self.far + j})

    def sum_core(self, m, b):
        src = b.g.at[:, self.half(1 - self.c), :]
        self.send(src, b.rc, self.r.gc_s.at[m], self.r.gc_r.at[m], {"dp": self.other})

    def sum_plane(self, m, b):
        self.arrive(b.rc, self.r.gc_s.at[m], self.r.gc_r.at[m], {"dp": self.other})

        def add(s):
            for i in range(2):
                rows = pl.ds(pl.multiple_of(self.c * HALF + i * 128, 128), 128)
                more = b.rc[s, pl.ds(i * 128, 128), :].astype(f32)
                b.g[s, rows, :] = (b.g[s, rows, :].astype(f32) + more).astype(bf16)

        loop(NMP, add)
        for j in range(1, self.nq):
            n = m * (self.nq - 1) + j - 1
            to = self.quarter(j)
            src = b.g.at[:, self.piece_rows(to), :]
            where = {"dp": 2 * to + self.c}
            self.send(src, b.rp.at[j - 1], self.r.gp_s.at[n], self.r.gp_r.at[n], where)

    def sum_z(self, m, b):
        for j in range(1, self.nq):
            n = m * (self.nq - 1) + j - 1
            where = {"dp": 2 * self.quarter(j) + self.c}
            self.arrive(b.rp.at[j - 1], self.r.gp_s.at[n], self.r.gp_r.at[n], where)
        for s in range(NMP):
            tot = b.g[s, self.piece_rows(self.q), :].astype(f32)
            for j in range(self.nq - 1):
                tot = tot + b.rp[j, s].astype(f32)
            b.pz[s] = tot.astype(bf16)
        for k in range(1, NMP):
            to = self.mp_peer(k)
            i = m * 3 + k - 1
            self.send(b.pz.at[to], b.rz.at[k - 1], self.r.gz_s.at[i], self.r.gz_r.at[i], {"mp": to})

    def sum_share(self, m, b):
        tot = b.pz[self.z].astype(f32)
        for k in range(1, NMP):
            i = m * 3 + k - 1
            where = {"mp": self.mp_peer(k)}
            self.arrive(b.rz.at[k - 1], self.r.gz_s.at[i], self.r.gz_r.at[i], where)
            tot = tot + b.rz[k - 1].astype(f32)
        mine = self.rows_of(self.me)
        b.fin[mine, :] = tot.astype(bf16)
        for k in range(1, self.ndp):
            n = m * (self.ndp - 1) + k - 1
            where = {"dp": self.dp_peer(k)}
            part = b.fin.at[mine, :]
            self.send(part, part, self.r.gs_s.at[n], self.r.gs_r.at[n], where)

    def sum_done(self, m, b):
        for k in range(1, self.ndp):
            n = m * (self.ndp - 1) + k - 1
            got = b.fin.at[self.rows_of(self.dp_peer(self.ndp - k)), :]
            where = {"dp": self.dp_peer(k)}
            self.arrive(got, self.r.gs_s.at[n], self.r.gs_r.at[n], where)

    def norms_z(self):
        r = self.r
        r.nz[self.z] = r.norms[...]
        for k in range(1, NMP):
            dst = r.nz.at[self.z]
            where = {"mp": self.mp_peer(k)}
            self.send(r.norms, dst, r.nz_s.at[k - 1], r.nz_r.at[k - 1], where)

    def norms_dp(self):
        r = self.r
        for k in range(1, NMP):
            got = r.nz.at[self.mp_peer(NMP - k)]
            self.arrive(got, r.nz_s.at[k - 1], r.nz_r.at[k - 1], {"mp": self.mp_peer(k)})
        tot = r.nz[0]
        for k in range(1, NMP):
            tot = tot + r.nz[k]
        r.np[self.me] = tot
        for k in range(1, self.ndp):
            dst = r.np.at[self.me]
            where = {"dp": self.dp_peer(k)}
            self.send(dst, dst, r.np_s.at[k - 1], r.np_r.at[k - 1], where)

    def norms_done(self):
        r = self.r
        for k in range(1, self.ndp):
            got = r.np.at[self.dp_peer(self.ndp - k)]
            self.arrive(got, r.np_s.at[k - 1], r.np_r.at[k - 1], {"dp": self.dp_peer(k)})
        tot = r.np[0]
        for k in range(1, self.ndp):
            tot = tot + r.np[k]
        r.onorm[...] = tot

    def finish(self):
        for copy in self.sent:
            copy.wait_send()


FAR_OUTS = ("oat", "oup", "odn")
NAMES = ("w0", "w1", "w2", "w3", "up", "dn")


def grad_buffers(r, n):
    get = lambda k: getattr(r, k + n)
    return types.SimpleNamespace(
        g=get("g"), rc=get("rc_"), rp=get("rp_"), pz=get("pz_"), rz=get("rz_"), fin=get("fin_")
    )


def whole_kernel(ndp, r):
    net = Links(r, ndp)
    z = net.z
    r.act, r.gp = r.big.at[pl.ds(0, T), :], r.big.at[pl.ds(T, T), :]
    r.dqe, r.dke, r.dve, r.ge = (r.big.at[:, pl.ds(i * D, D)] for i in range(4))
    bufs = [grad_buffers(r, n) for n in NAMES]
    loads = []
    for i, w in enumerate((r.w_query, r.w_key, r.w_value)):
        dst = r.wat.at[z, :, pl.ds(i * 128, 128)]
        loads.append(pltpu.make_async_copy(w, dst, r.ld.at[i]))
    loads.append(pltpu.make_async_copy(r.w_up, r.wup.at[z], r.ld.at[3]))
    loads.append(pltpu.make_async_copy(r.w_down, r.wdn.at[z], r.ld.at[4]))
    for copy in loads:
        copy.start()
    net.barrier()
    r.wat[z, :, pl.ds(384, 128)] = r.w_output[...].T
    for copy in loads[:3]:
        copy.wait()
    net.gather_z(0, r.wat)
    for copy in loads[3:]:
        copy.wait()
    net.gather_z(1, r.wup)
    net.gather_z(2, r.wdn)
    r.norms[...] = jnp.zeros_like(r.norms)
    norm_one(r)
    net.gather_plane(0, r.wat)
    build_tables(r, z)
    build_maps(r)
    net.gather_core(0, r.wat)
    net.gather_done(0, r.wat)
    project(r, z, 0)
    net.gather_plane(1, r.wup)
    project(r, z, 1)
    net.gather_plane(2, r.wdn)
    pool_levels(r, z)
    net.coarse_send()
    loop(4, lambda c: attend_chunk(r, c))
    net.gather_core(1, r.wup)
    net.gather_core(2, r.wdn)
    loop(3, lambda c: attend_chunk(r, c + 4))
    net.coarse_wait()
    place_remote(r)
    attend_chunk(r, EXT // 128 - 1)
    combine_sums(r)
    combine_values(r)
    attn_out(r)
    net.gather_done(1, r.wup)
    net.gather_done(2, r.wdn)
    ffn_inner(r)
    down_grads(r)
    net.sum_core(5, bufs[5])
    up_grads(r)
    net.sum_core(4, bufs[4])
    net.sum_plane(5, bufs[5])
    ffn_outer(r)
    net.sum_plane(4, bufs[4])
    out_grads(r)
    net.sum_core(3, bufs[3])
    attn_back_rows(r)
    net.sum_z(5, bufs[5])
    net.sum_plane(3, bufs[3])
    attend_back_chunk(r, EXT // 128 - 1, False)
    save_remote(r)
    net.coarse_back()
    loop(2, lambda c: attend_back_chunk(r, c, True))
    net.sum_share(5, bufs[5])
    net.sum_z(4, bufs[4])
    loop(2, lambda c: attend_back_chunk(r, c + 2, True))
    net.sum_share(4, bufs[4])
    net.sum_z(3, bufs[3])
    loop(3, lambda c: attend_back_chunk(r, c + 4, False))
    net.sum_share(3, bufs[3])
    net.coarse_back_wait()
    unpool_values(r, z)
    weight_grad(r, r.gw2, r.ve)
    net.sum_core(2, bufs[2])
    unpool_keys(r, z)
    weight_grad(r, r.gw1, r.ke)
    net.sum_core(1, bufs[1])
    net.sum_plane(2, bufs[2])
    unpool_queries(r, z)
    weight_grad(r, r.gw0, r.qe)
    net.sum_core(0, bufs[0])
    net.sum_plane(1, bufs[1])
    input_grads(r, 0)
    net.sum_plane(0, bufs[0])
    net.sum_z(2, bufs[2])
    input_grads(r, 1)
    net.sum_z(1, bufs[1])
    input_grads(r, 2)
    net.sum_share(2, bufs[2])
    net.sum_z(0, bufs[0])
    input_grads(r, 3)
    net.norms_z()
    net.sum_share(1, bufs[1])
    net.sum_share(0, bufs[0])
    net.norms_dp()
    places = [r.oat.at[:, pl.ds(i * 128, 128)] for i in range(4)] + [r.oup, r.odn]
    stores = []
    for m in (5, 4, 3, 2, 1, 0):
        net.sum_done(m, bufs[m])
        stores.append(pltpu.make_async_copy(bufs[m].fin, places[m], r.st.at[m]))
        stores[-1].start()
    net.norms_done()
    for copy in stores:
        copy.wait()
    net.finish()


def run(body, ins, outs, scratch, sems):
    names = list(ins) + list(outs) + list(scratch) + list(sems)

    def kernel(*refs):
        body(types.SimpleNamespace(**dict(zip(names, refs))))

    result = pl.pallas_call(
        kernel,
        out_shape=[jax.ShapeDtypeStruct(*v) for v in outs.values()],
        in_specs=[pl.BlockSpec(memory_space=space) for _, space in ins.values()],
        out_specs=[
            pl.BlockSpec(memory_space=pl.ANY if n in FAR_OUTS else pltpu.VMEM) for n in outs
        ],
        scratch_shapes=[pltpu.VMEM(*v) for v in scratch.values()]
        + [pltpu.SemaphoreType.DMA((n,)) for n in sems.values()],
        compiler_params=pltpu.CompilerParams(
            vmem_limit_bytes=63 * 1024 * 1024, collective_id=0, has_side_effects=True
        ),
    )(*[a for a, _ in ins.values()])
    return dict(zip(outs, result))


def per_device(
    ndp,
    tokens,
    lengths,
    gain_one,
    shift_one,
    w_query,
    w_key,
    w_value,
    w_output,
    gain_two,
    shift_two,
    w_up,
    w_down,
    cotangent,
):
    x = jnp.swapaxes(tokens, 0, 1).reshape(T, D)
    gy = jnp.swapaxes(cotangent, 0, 1).reshape(T, D)
    g1, b1, g2, b2 = (v.reshape(1, D) for v in (gain_one, shift_one, gain_two, shift_two))
    nq, piece = ndp // 2, LOC // ndp
    vmem, any_space = pltpu.VMEM, pl.ANY
    ins = dict(
        lens=(lengths, pltpu.SMEM),
        x=(x, vmem),
        gy=(gy, vmem),
        g1=(g1, vmem),
        b1=(b1, vmem),
        g2=(g2, vmem),
        b2=(b2, vmem),
        w_query=(w_query, any_space),
        w_key=(w_key, any_space),
        w_value=(w_value, any_space),
        w_output=(w_output, vmem),
        w_up=(w_up, any_space),
        w_down=(w_down, any_space),
    )
    outs = dict(
        mixed=((T, D), bf16),
        gx=((T, D), f32),
        oat=((D, 512), bf16),
        oup=((D, 512), bf16),
        odn=((512, D), bf16),
        onorm=((8, D), f32),
    )
    scratch = dict(
        wat=((NMP, D, 512), bf16),
        wup=((NMP, D, 512), bf16),
        wdn=((NMP, 512, D), bf16),
        h1=((T, D), bf16),
        qe=((ND * EXT, D), bf16),
        ke=((ND * EXT, D), bf16),
        ve=((ND * EXT, D), bf16),
        pool=((EXT - LOC, LOC), bf16),
        unpool=((LOC, EXT - LOC), bf16),
        cc=((ND * EXT, 128), bf16),
        bias=((ND * EXT, 128), f32),
        wts=((64 * 128, 256), bf16),
        num=((ND * EXT, D), f32),
        tops=((EXT, 128), f32),
        sumz=((EXT, 128), f32),
        up=((LOC, 128), f32),
        up2=((LOC, 128), f32),
        fa=((EXT, 128), f32),
        fb=((EXT, 128), f32),
        ctx=((T, D), bf16),
        h2=((T, D), bf16),
        big=((2 * T, FF), bf16),
        gm=((T, D), bf16),
        hc=((T // 2, D), f32),
        dl=((EXT, 128), f32),
        ee=((ND, 256, D), bf16),
        crow=((ND * EXT // 128, 128), f32),
        sums=((2 * ND, 24, D), f32),
        rem=((2 * ND, 32, D), f32),
        back=((2 * ND, 32, D), f32),
        near=((2 * ND, 16, D), f32),
        far=((2, 2 * ND, 8, D), f32),
        norms=((8, D), f32),
        nz=((NMP, 8, D), f32),
        np=((ndp, 8, D), f32),
    )
    for n in NAMES:
        cols = 512 if n in ("up", "dn") else 128
        scratch["g" + n] = ((NMP, 512, cols), bf16)
        scratch["rc_" + n] = ((NMP, HALF, cols), bf16)
        scratch["rp_" + n] = ((nq - 1, NMP, piece, cols), bf16)
        scratch["pz_" + n] = ((NMP, piece, cols), bf16)
        scratch["rz_" + n] = ((3, piece, cols), bf16)
        scratch["fin_" + n] = ((512, cols), bf16)
    counts = dict(
        wz=9, wp=9 * (nq - 1), wc=9, cf=3, cb=3, gc=6, gp=6 * (nq - 1), gz=18, gs=6 * (ndp - 1),
        nz=3, np=ndp - 1,
    )
    sems = dict(ld=5, st=6)
    for n, count in counts.items():
        sems[n + "_s"] = count
        sems[n + "_r"] = count
    o = run(lambda r: whole_kernel(ndp, r), ins, outs, scratch, sems)

    def back_to(a):
        return jnp.swapaxes(a.reshape(ND, LOC, D), 0, 1)

    at = [o["oat"][:, i * 128 : (i + 1) * 128].astype(f32) for i in range(4)]
    return (
        back_to(o["mixed"]),
        back_to(o["gx"]),
        at[0],
        at[1],
        at[2],
        at[3].T,
        o["oup"].astype(f32),
        o["odn"].astype(f32),
        *(o["onorm"][i] for i in range(4)),
    )


def solution(mesh):
    tok = P("mp", "dp", None)
    col, row, rep = P(None, "mp"), P("mp", None), P()
    ndp = mesh.shape["dp"]
    return jax.shard_map(
        lambda *args: per_device(ndp, *args),
        mesh=mesh,
        in_specs=(tok, P("dp"), rep, rep, col, col, col, row, rep, rep, col, row, tok),
        out_specs=(tok, tok, col, col, col, row, col, row, rep, rep, rep, rep),
        check_vma=False,
    )
```

```python
import types

import jax
import jax.numpy as jnp
from jax import lax
from jax.experimental import pallas as pl
from jax.experimental.pallas import tpu as pltpu
from jax.sharding import PartitionSpec as P

HD = 64
BLK = 16
NEG = -1e30
FLOOR = -1e29
EPS = 1e-05
LOC = 512
ND = 2
D = 512
FF = 2048
NMP = 4
HALF = 256
T = ND * LOC
HEADS = D // HD
LEVELS = 7
LOCAL_LEVELS = 5
EXT = 1024
RT = 512
G = [LOC >> lev for lev in range(LEVELS)]
OFF = [sum(G[:lev]) for lev in range(LEVELS)]
bf16 = jnp.bfloat16
f32 = jnp.float32
i32 = jnp.int32


def dot(a, b, ca=1, cb=0):
    return lax.dot_general(a, b, (((ca,), (cb,)), ((), ())), preferred_element_type=f32)


def iota(shape, axis):
    return lax.broadcasted_iota(i32, shape, axis)


def loop(n, body):
    lax.fori_loop(0, n, lambda i, c: (body(i), c)[1], 0)


def rows_at(i, size):
    return pl.ds(pl.multiple_of(i * size, size), size)


def own_groups(e):
    size = jnp.zeros_like(e)
    start = jnp.zeros_like(e)
    for lev in range(LEVELS):
        here = (e >= OFF[lev]) & (e < OFF[lev] + G[lev])
        size = jnp.where(here, 1 << lev, size)
        start = jnp.where(here, (e - OFF[lev]) << lev, start)
    return size, start


def key_groups(e, z):
    size, start = own_groups(e)
    start = start + z * LOC
    near = z + 1 - 2 * lax.rem(z, 2)
    far = 1 - z // 2
    size = jnp.where(e >= OFF[5], 32, size)
    start = jnp.where(e >= OFF[5], near * LOC + (e - OFF[5]) * 32, start)
    size = jnp.where(e >= OFF[6], 64, size)
    start = jnp.where(e >= OFF[6], far * 2 * LOC + (e - OFF[6]) * 64, start)
    return size, start


def count_live(size, start, length):
    return jnp.clip(length - start, 0, size).astype(f32)


def build_tables(r, z, d):
    r.ee[d] = head_map(d)
    length = r.lens[d]
    inv, inv_size = inv_counts(r, z, d)
    r.inv[d] = inv
    r.inv[ND] = inv_size

    def chunk(c):
        at = pl.ds(pl.multiple_of(d * EXT + c * 128, 128), 128)
        e_col = iota((128, 128), 0) + c * 128
        size, start = key_groups(e_col, z)
        r.cc[at, :] = count_live(size, start, length).astype(bf16)
        e_row = iota((1, 128), 1) + c * 128
        size, start = key_groups(e_row, z)
        dead = count_live(size, start, length)
        r.crow[pl.ds(d * (EXT // 128) + c, 1), :] = dead
        q_blk, k_blk = e_col // BLK, jnp.broadcast_to(e_row // BLK, (128, 128))
        span = jnp.where(q_blk // 2 == k_blk // 2, 0.0, NEG)
        same = jnp.where(q_blk == k_blk, 0.0, NEG)
        cross = jnp.where(q_blk == k_blk, NEG, span)
        bias = jnp.where(e_col < LOC, span, jnp.where(e_col < OFF[5], cross, same))
        r.bias[at, :] = jnp.where(jnp.broadcast_to(dead, (128, 128)) > 0.0, bias, NEG).astype(bf16)

    loop(EXT // 128, chunk)


def build_maps(r):
    def tile(c):
        rows = rows_at(c, 128)
        size, start = own_groups(iota((128, LOC), 0) + c * 128 + LOC)
        pos = iota((128, LOC), 1)
        r.pool[rows, :] = ((pos >= start) & (pos < start + size)).astype(f32).astype(bf16)
        size, start = own_groups(iota((128, EXT - LOC), 1) + LOC)
        pos = iota((128, EXT - LOC), 0) + c * 128
        r.unpool[rows, :] = ((pos >= start) & (pos < start + size)).astype(f32).astype(bf16)

    loop((EXT - LOC) // 128, tile)


def inv_counts(r, z, d):
    e = iota((EXT - LOC, 128), 0) + LOC
    size, start = own_groups(e)
    cnt = count_live(size, start + z * LOC, r.lens[d])
    return 1.0 / jnp.maximum(cnt, 1.0), 1.0 / jnp.maximum(size, 1).astype(f32)


def wide(col):
    return jnp.concatenate([col] * (D // 128), axis=1)


def live_rows(r, z, d, first, count):
    pos = iota((count, D), 0) + first + z * LOC
    return pos < r.lens[d]


def stats(v):
    mean = jnp.mean(v, axis=-1, keepdims=True)
    cen = v - mean
    var = jnp.mean(cen * cen, axis=-1, keepdims=True)
    return cen, lax.rsqrt(var + EPS)


def by_document(dst, raw):
    def tile(t):
        v = raw[rows_at(t, 128)].astype(f32)
        for d in range(ND):
            at = pl.ds(pl.multiple_of(d * LOC + t * 128, 128), 128)
            dst[at, :] = v[:, d, :].astype(bf16)

    loop(LOC // 128, tile)


def norm_one(r):
    r.tops[...] = jnp.zeros_like(r.tops)
    r.sumz[...] = jnp.zeros_like(r.sumz)
    r.norms[...] = jnp.zeros_like(r.norms)

    def tile(t):
        rows = rows_at(t, RT)
        cen, rstd = stats(r.x[rows, :].astype(f32))
        r.h1[rows, :] = (cen * rstd * r.g1[...] + r.b1[...]).astype(bf16)

    loop(T // RT, tile)


def ext_rows(d, off, count):
    return pl.ds(d * EXT + off, count)


def attn_weight(r, t):
    return jnp.concatenate([r.wat[s, :, t * 128 : (t + 1) * 128] for s in range(NMP)], axis=1)


def pair_lanes(s):
    return pl.ds(pl.multiple_of(s * 128, 128), 128)


def project(r, z, shards):
    for d in range(ND):

        def tile(t, d=d):
            rows = pl.ds(pl.multiple_of(d * LOC + t * RT, RT), RT)
            at = pl.ds(pl.multiple_of(d * EXT + t * RT, RT), RT)
            w = [r.wat[s, :, 0:384] for s in shards]
            o = dot(r.h1[rows, :], jnp.concatenate(w, axis=1))
            live = iota((RT, 128), 0) + t * RT + z * LOC < r.lens[d]
            for i, s in enumerate(shards):
                lanes = pair_lanes(s)
                q, k, v = (o[:, i * 384 + j * 128 : i * 384 + (j + 1) * 128] for j in range(3))
                r.qe[at, lanes] = (q.astype(bf16).astype(f32) * (HD**-0.5)).astype(bf16)
                r.ke[at, lanes] = jnp.where(live, k, 0.0).astype(bf16)
                r.ve[at, lanes] = jnp.where(live, v, 0.0).astype(bf16)

        loop(LOC // RT, tile)


def pool_levels(r, shards):
    keep = OFF[5] - LOC
    for d in range(ND):
        fine = ext_rows(d, 0, LOC)
        x = [e[fine, pair_lanes(s)] for s in shards for e in (r.qe, r.ke, r.ve)]
        o = dot(r.pool[...], jnp.concatenate(x, axis=1))
        for i, s in enumerate(shards):
            lanes = pair_lanes(s)
            q, k, v = (o[:, i * 384 + j * 128 : i * 384 + (j + 1) * 128] for j in range(3))
            r.qe[ext_rows(d, LOC, LOC), lanes] = (q * r.inv[ND]).astype(bf16)
            k = k * r.inv[d]
            r.ke[ext_rows(d, LOC, keep), lanes] = k[:keep].astype(bf16)
            r.ve[ext_rows(d, LOC, keep), lanes] = v[:keep].astype(bf16)
            r.out5[2 * d, :, lanes] = k[keep : keep + 16].astype(bf16)
            r.out5[2 * d + 1, :, lanes] = v[keep : keep + 16].astype(bf16)
            last = [k[keep + 16 : keep + 24], v[keep + 16 : keep + 24]]
            r.out6[d, :, lanes] = jnp.concatenate(last, axis=0).astype(bf16)


def place_remote(r):
    for d in range(ND):
        for kv, e in enumerate((r.ke, r.ve)):
            far = [r.in6[j, d].astype(f32)[kv * 8 : kv * 8 + 8] for j in range(2)]
            e[ext_rows(d, OFF[5], 16), :] = r.in5[2 * d + kv]
            e[ext_rows(d, OFF[6], 16), :] = jnp.concatenate(far, axis=0).astype(bf16)


def split_heads(pair):
    first = iota(pair.shape, 1) < HD
    zero = jnp.zeros_like(pair)
    return jnp.concatenate([jnp.where(first, pair, zero), jnp.where(first, zero, pair)], axis=0)


def count_lanes(cc, d, p):
    lane = iota(cc.shape, 1)
    zero = jnp.zeros_like(cc)
    a = jnp.where(lane == d * HEADS + 2 * p, cc, zero)
    b = jnp.where(lane == d * HEADS + 2 * p + 1, cc, zero)
    return jnp.concatenate([a, b], axis=0)


def attend_step(r, c, d, s, tops, sums):
    lane = iota((128, 128), 1)
    at = pl.ds(pl.multiple_of(d * EXT + c * 128, 128), 128)
    bias = r.bias[at, :].astype(f32)
    lanes = pair_lanes(s)
    w = dot(r.qe[at, lanes], split_heads(r.ke[at, lanes]), 1, 1)
    parts = []
    for j in range(2):
        sj = w[:, j * 128 : (j + 1) * 128] + bias
        top = jnp.maximum(jnp.max(sj, axis=1, keepdims=True), FLOOR)
        parts.append(jnp.exp(sj - top))
        tops = jnp.where(lane == d * HEADS + 2 * s + j, top, tops)
    e = jnp.concatenate(parts, axis=1).astype(bf16)
    r.wts[pl.ds(pl.multiple_of(((c * ND + d) * 4 + s) * 128, 128), 128), :] = e
    cnt = count_lanes(r.cc[at, :], d, s)
    o = dot(e, jnp.concatenate([split_heads(r.ve[at, lanes]), cnt], axis=1))
    r.num[at, lanes] = o[:, :128]
    return tops, sums + o[:, 128:]


def attend_chunk(r, c, pairs):
    here = rows_at(c, 128)
    tops, sums = r.tops[here, :], r.sumz[here, :]
    for s in pairs:
        for d in range(ND):
            tops, sums = attend_step(r, c, d, s, tops, sums)
    r.tops[here, :] = tops
    r.sumz[here, :] = sums


def attend_own(r, s):
    def two(i):
        attend_chunk(r, 2 * i, (s,))
        attend_chunk(r, 2 * i + 1, (s,))

    loop(3, two)
    attend_chunk(r, 6, (s,))


def combine_sums(r):
    last = pl.ds(OFF[6], G[6])
    top = r.tops[last, :]
    tot = r.sumz[last, :]
    for lev in range(LEVELS - 2, -1, -1):
        n = G[lev]
        for half in range(2):
            r.up[pl.ds(half, n // 2, stride=2), :] = top
            r.up2[pl.ds(half, n // 2, stride=2), :] = tot
        at = pl.ds(OFF[lev], n)
        up_top = r.up[pl.ds(0, n), :]
        own = r.tops[at, :]
        top = jnp.maximum(own, up_top)
        a = jnp.exp(own - top)
        b = jnp.exp(up_top - top)
        tot = a * r.sumz[at, :] + b * r.up2[pl.ds(0, n), :]
        if lev == 0:
            used = iota(tot.shape, 1) < ND * HEADS
            inv = 1.0 / jnp.where(used, tot, 1.0)
            a, b = a * inv, b * inv
        r.fa[at, :] = a
        r.fb[at, :] = b


def high_low(v, axis):
    hi = v.astype(bf16).astype(f32)
    return jnp.concatenate([hi, v - hi], axis=axis).astype(bf16)


def spread(r, fac, d):
    return dot(high_low(fac, 1), r.ee[d])


def head_map(d):
    row = lax.rem(iota((256, D), 0), 128)
    return (row == d * HEADS + iota((256, D), 1) // HD).astype(f32).astype(bf16)


def up_map(n):
    return (iota((n, n), 0) // 2 == lax.rem(iota((n, n), 1), n // 2)).astype(f32).astype(bf16)


def down_map(n):
    return (lax.rem(iota((2 * n, n // 2), 0), n) // 2 == iota((2 * n, n // 2), 1)).astype(f32).astype(bf16)


def combine_values(r):
    for d in range(ND):
        cur = r.num[ext_rows(d, OFF[6], G[6]), :]
        for lev in range(LEVELS - 2, -1, -1):
            n = G[lev]
            parts = []
            step = min(n, 256)
            for t in range(n // step):
                at = pl.ds(OFF[lev] + t * step, step)
                here = ext_rows(d, OFF[lev] + t * step, step)
                fac = spread(r, jnp.concatenate([r.fa[at, :], r.fb[at, :]], axis=0), d)
                up = dot(up_map(step), high_low(cur[t * step // 2 : (t + 1) * step // 2], 0))
                parts.append(fac[:step] * r.num[here, :] + fac[step:] * up)
                if lev == 0:
                    r.ctx[pl.ds(d * LOC + t * step, step), :] = parts[-1].astype(bf16)
                    r.num[here, :] = parts[-1]
            cur = jnp.concatenate(parts, axis=0) if len(parts) > 1 else parts[0]


def spare_rows(t):
    per = LOC // RT
    return pl.ds(pl.multiple_of((t // per) * EXT + LOC + lax.rem(t, per) * RT, RT), RT)


def attn_out(r):
    def tile(t):
        rows = rows_at(t, RT)
        mid = r.x[rows, :].astype(f32) + dot(r.ctx[rows, :], attn_weight(r, 3), 1, 1)
        r.num[spare_rows(t), :] = mid
        cen, rstd = stats(mid)
        r.h2[rows, :] = (cen * rstd * r.g2[...] + r.b2[...]).astype(bf16)

    loop(T // RT, tile)


def ffn_inner(r, f):
    cols = rows_at(f, 512)
    n = 256
    for t in range(T // n):
        rows = pl.ds(t * n, n)
        pre = dot(r.h2[rows, :], r.wup[f])
        ga = dot(r.gy[rows, :], r.wdn[f], 1, 1)
        cdf = 0.5 + 0.5 * lax.erf(pre * (0.5**0.5))
        r.act[rows, cols] = (pre * cdf).astype(bf16)
        pdf = jnp.exp(pre * pre * -0.5) * 0.3989422804014327
        r.gp[rows, cols] = (ga * (cdf + pre * pdf)).astype(bf16)


def ffn_grads(r, f, k):
    cols = rows_at(f, 512)
    r.f_g[k, 0] = dot(r.h2[...], r.gp[:, cols], 0, 0).astype(bf16)
    r.f_g[k, 1] = dot(r.act[:, cols], r.gy[...], 0, 0).astype(bf16)


def norm_back(v, gain, gh, r, row):
    cen, rstd = stats(v)
    xhat = cen * rstd
    r.norms[row : row + 1, :] += jnp.sum(gh * xhat, axis=0, keepdims=True)
    r.norms[row + 1 : row + 2, :] += jnp.sum(gh, axis=0, keepdims=True)
    u = gh * gain
    return rstd * (
        u - jnp.mean(u, axis=-1, keepdims=True) - xhat * jnp.mean(u * xhat, axis=-1, keepdims=True)
    )


def ffn_outer(r, t):
    rows = rows_at(t, RT)
    mid = r.num[spare_rows(t), :]
    ffn = dot(r.act[rows, 0:512], r.wdn[0])
    gh2 = dot(r.gp[rows, 0:512], r.wup[0], 1, 1)
    for f in range(1, NMP):
        cols = slice(f * 512, (f + 1) * 512)
        ffn = ffn + dot(r.act[rows, cols], r.wdn[f])
        gh2 = gh2 + dot(r.gp[rows, cols], r.wup[f], 1, 1)
    r.mx[rows, :] = (mid + ffn).astype(bf16)
    g_mid = r.gy[rows, :].astype(f32) + norm_back(mid, r.g2[...], gh2, r, 2)
    r.gxs[rows, :] = g_mid
    r.gm[rows, :] = g_mid.astype(bf16)


def out_grads(r, z):
    r.gof[...] = dot(r.gm[...], r.ctx[...], 0, 0).astype(bf16)
    for k in range(NMP):
        r.o_g[k, 0] = r.gof[:, pair_lanes(shard_of(z, k))]


def at_lanes(base, s):
    return pl.ds(pl.multiple_of(base + s * 128, 128), 128)


def store_pair(r, d, off, count, v):
    hi = v.astype(bf16)
    r.act[pl.ds(off, count), d * D : (d + 1) * D] = hi
    r.act[pl.ds(off, count), (ND + d) * D : (ND + d + 1) * D] = (v - hi.astype(f32)).astype(bf16)


def context_grads(r):
    def tile(t):
        r.num[spare_rows(t), :] = dot(r.gm[rows_at(t, RT), :], attn_weight(r, 3))

    loop(T // RT, tile)


def attn_back_rows(r):
    lane_head = lax.rem(iota((2 * D, 128), 0), D) // HD
    n = 256
    for t in range(LOC // n):
        at = pl.ds(t * n, n)
        delta = jnp.zeros((n, 128), f32)
        for d in range(ND):
            gctx = r.num[ext_rows(d, LOC + t * n, n), :]
            sel = (lane_head + d * HEADS == iota((2 * D, 128), 1)).astype(f32).astype(bf16)
            delta = delta + dot(high_low(gctx * r.num[ext_rows(d, t * n, n), :], 1), sel)
            fac = spread(r, jnp.concatenate([r.fa[at, :], r.fb[at, :]], axis=0), d)
            store_pair(r, d, t * n, n, fac[:n] * gctx)
            down = high_low(fac[n:] * gctx, 0)
            r.hc[pl.ds((d * LOC + t * n) // 2, n // 2), :] = dot(down_map(n), down, 0, 0)
        r.dl[at, :] = r.fa[at, :] * delta
        r.up[at, :] = r.fb[at, :] * delta
    acc = r.up[pl.ds(0, LOC // 2, stride=2), :] + r.up[pl.ds(1, LOC // 2, stride=2), :]
    for lev in range(1, LEVELS - 1):
        n = G[lev]
        at = pl.ds(OFF[lev], n)
        r.dl[at, :] = r.fa[at, :] * acc
        r.up[pl.ds(0, n), :] = r.fb[at, :] * acc
        acc = r.up[pl.ds(0, n // 2, stride=2), :] + r.up[pl.ds(1, n // 2, stride=2), :]
    r.dl[pl.ds(OFF[6], 2 * G[6]), :] = jnp.concatenate([acc, jnp.zeros_like(acc)], 0)
    for d in range(ND):
        cur = r.hc[pl.ds(d * LOC // 2, LOC // 2), :]
        for lev in range(1, LEVELS - 1):
            n = G[lev]
            parts = []
            step = min(n, 256)
            for t in range(n // step):
                at = pl.ds(OFF[lev] + t * step, step)
                seg = cur[t * step : (t + 1) * step]
                fac = spread(r, jnp.concatenate([r.fa[at, :], r.fb[at, :]], axis=0), d)
                store_pair(r, d, OFF[lev] + t * step, step, fac[:step] * seg)
                down = high_low(fac[step:] * seg, 0)
                parts.append(dot(down_map(step), down, 0, 0))
            cur = jnp.concatenate(parts, axis=0) if len(parts) > 1 else parts[0]
        store_pair(r, d, OFF[6], 2 * G[6], jnp.concatenate([cur, jnp.zeros_like(cur)], axis=0))


def attend_back_step(r, c, fine, s, d):
    top = iota((128, 128), 0) < HD
    lane = iota((128, 128), 1)
    lanes = pair_lanes(s)
    rows = rows_at(c, 128)
    dl = r.dl[rows, :]
    at = pl.ds(pl.multiple_of(d * EXT + c * 128, 128), 128)
    cnt = jnp.broadcast_to(r.crow[pl.ds(d * (EXT // 128) + c, 1), :], (128, 128))
    g = r.act[rows, at_lanes(d * D, s)]
    low = r.act[rows, at_lanes((ND + d) * D, s)]
    q = r.qe[at, lanes]
    kcat = split_heads(r.ke[at, lanes])
    vcat = split_heads(r.ve[at, lanes])
    dp = dot(jnp.concatenate([g, low], axis=1), jnp.concatenate([vcat, vcat], axis=1), 1, 1)
    e = r.wts[pl.ds(pl.multiple_of(((c * ND + d) * 4 + s) * 128, 128), 128), :]
    parts = []
    for j in range(2):
        half = slice(j * 128, (j + 1) * 128)
        mine = jnp.where(lane == d * HEADS + 2 * s + j, dl, 0.0)
        delta = jnp.sum(mine, axis=1, keepdims=True)
        parts.append(e[:, half].astype(f32) * (dp[:, half] - delta * cnt))
    ds = jnp.concatenate(parts, axis=1).astype(bf16)
    dq = dot(ds, kcat)
    dk = dot(q, ds, 0, 0)
    dk = jnp.where(top, dk[:, :128], dk[:, 128:]).T
    if fine:
        r.num[at, lanes] = dq
        r.num[pl.ds(pl.multiple_of(d * EXT + LOC + c * 128, 128), 128), lanes] = dk
    else:
        coarse = at_lanes((ND + d) * D, s)
        r.gp[rows_at(c - LOC // 128, 128), coarse] = dq.astype(bf16)
        r.gp[rows_at(c, 128), coarse] = dk.astype(bf16)


def attend_back_chunk(r, c, fine, pairs):
    for s in pairs:
        for d in range(ND):
            attend_back_step(r, c, fine, s, d)


def values_back(r, c, s):
    top = iota((128, 128), 0) < HD
    rows = rows_at(c, 128)
    for d in range(ND):
        g = r.act[rows, at_lanes(d * D, s)]
        slot = pl.ds(pl.multiple_of(((c * ND + d) * 4 + s) * 128, 128), 128)
        dv = dot(g, r.wts[slot, :], 0, 0)
        r.gp[rows, at_lanes(d * D, s)] = jnp.where(top, dv[:, :128], dv[:, 128:]).T.astype(bf16)


def attend_back_pair(r, s):
    for c in range(4):
        attend_back_chunk(r, c, True, (s,))
    for c in range(4, 7):
        attend_back_chunk(r, c, False, (s,))
    for c in range(7):
        values_back(r, c, s)


def coarse_grad(r, kv, d, first, count, cols):
    base = d * D if kv else (ND + d) * D
    if cols is None:
        return r.gp[pl.ds(first, count), base : base + D]
    return r.gp[pl.ds(first, count), at_lanes(base, cols)]


def save_remote(r):
    for d in range(ND):
        last = []
        for kv in range(2):
            r.out5[2 * d + kv] = coarse_grad(r, kv, d, OFF[5], 16, None)
            last.append(coarse_grad(r, kv, d, OFF[6], 16, None).astype(f32))
        for j in range(2):
            rows = [v[j * 8 : j * 8 + 8] for v in last]
            r.back6[j, d] = jnp.concatenate(rows, axis=0).astype(bf16)


def coarse_rows(r, d, kv, s):
    keep = OFF[5] - LOC
    own = coarse_grad(r, kv, d, LOC, keep, s).astype(f32)
    lanes = pair_lanes(s)
    rest = jnp.zeros((LOC - keep - 24, 128), f32)
    far = r.far6[0, d, :, lanes].astype(f32) + r.far6[1, d, :, lanes].astype(f32)
    near = r.near5[2 * d + kv, :, lanes].astype(f32)
    return jnp.concatenate([own, near, far[kv * 8 : kv * 8 + 8], rest], axis=0)


def unpool(r, z, s):
    lanes = pair_lanes(s)
    for d in range(ND):
        q = r.gp[pl.ds(0, LOC), at_lanes((ND + d) * D, s)].astype(f32) * r.inv[ND]
        k = coarse_rows(r, d, 0, s) * r.inv[d]
        v = coarse_rows(r, d, 1, s)
        o = dot(r.unpool[...], jnp.concatenate([q, k, v], axis=1).astype(bf16))
        rows = pl.ds(d * LOC, LOC)
        fine = ext_rows(d, 0, LOC)
        live = iota((LOC, 128), 0) + z * LOC < r.lens[d]
        q = r.num[fine, lanes] + o[:, :128]
        r.gq[rows, lanes] = (q * (HD**-0.5)).astype(bf16)
        k = r.num[ext_rows(d, LOC, LOC), lanes] + o[:, 128:256]
        r.gk[rows, lanes] = jnp.where(live, k, 0.0).astype(bf16)
        v = r.gp[pl.ds(0, LOC), at_lanes(d * D, s)].astype(f32) + o[:, 256:]
        r.gv[rows, lanes] = jnp.where(live, v, 0.0).astype(bf16)


def attn_grads(r, s, k):
    lanes = pair_lanes(s)
    g = jnp.concatenate([r.gq[:, lanes], r.gk[:, lanes], r.gv[:, lanes]], axis=1)
    r.a_g[k, 0] = dot(r.h1[...], g, 0, 0).astype(bf16)


def input_grads(r, t):
    rows = rows_at(t, RT)
    gh1 = dot(r.gq[rows, :], attn_weight(r, 0), 1, 1)
    gh1 = gh1 + dot(r.gk[rows, :], attn_weight(r, 1), 1, 1)
    gh1 = gh1 + dot(r.gv[rows, :], attn_weight(r, 2), 1, 1)
    x = r.x[rows, :].astype(f32)
    r.gxs[rows, :] = r.gxs[rows, :] + norm_back(x, r.g1[...], gh1, r, 0)


def shard_of(z, k):
    return lax.rem(z + NMP - k, NMP)


def remote(src, dst, send, recv, where):
    return pltpu.make_async_remote_copy(
        src_ref=src, dst_ref=dst, send_sem=send, recv_sem=recv, device_id=where,
        device_id_type=pl.DeviceIdType.MESH,
    )


class Links:
    def __init__(self, r, ndp):
        self.r, self.ndp, self.nq, self.piece = r, ndp, ndp // 2, LOC // ndp
        self.z, self.me = lax.axis_index("mp"), lax.axis_index("dp")
        self.c, self.q = lax.rem(self.me, 2), self.me // 2
        self.other = 2 * self.q + 1 - self.c
        self.near = self.z + 1 - 2 * lax.rem(self.z, 2)
        self.far = (1 - self.z // 2) * 2
        self.par = lax.rem(self.z, 2)
        self.sent = []

    def mp_peer(self, k):
        return lax.rem(self.z + k, NMP)

    def dp_peer(self, k):
        return lax.rem(self.me + k, self.ndp)

    def quarter(self, j):
        return lax.rem(self.q + j, self.nq)

    def piece_rows(self, q):
        return pl.ds(pl.multiple_of(self.c * HALF + q * self.piece, self.piece), self.piece)

    def rows_of(self, dev):
        first = lax.rem(dev, 2) * HALF + (dev // 2) * self.piece
        return pl.ds(pl.multiple_of(first, self.piece), self.piece)

    def half(self, c):
        return pl.ds(pl.multiple_of(c * HALF, HALF), HALF)

    def send(self, src, dst, send, recv, where):
        copy = remote(src, dst, send, recv, where)
        copy.start()
        self.sent.append(copy)

    def arrive(self, dst, send, recv, where):
        remote(dst, dst, send, recv, where).wait_recv()

    def greet(self):
        sem = pltpu.get_barrier_semaphore()
        for k in range(1, NMP):
            pl.semaphore_signal(sem, inc=1, device_id={"mp": self.mp_peer(k)})
        for k in range(1, self.ndp):
            pl.semaphore_signal(sem, inc=1, device_id={"dp": self.dp_peer(k)})

    def barrier(self):
        pl.semaphore_wait(pltpu.get_barrier_semaphore(), NMP + self.ndp - 2)

    def gather_z(self, m, k):
        w, cols = self.weights[m]
        i = m * 3 + k - 1
        piece = w.at[self.z, self.rows_of(self.me), cols]
        self.send(piece, piece, self.r.wz_s.at[i], self.r.wz_r.at[i], {"mp": self.mp_peer(k)})

    def gather_plane(self, m, k):
        w, cols = self.weights[m]
        i = m * 3 + k - 1
        piece = w.at[shard_of(self.z, k), self.rows_of(self.me), cols]
        self.arrive(piece, self.r.wz_s.at[i], self.r.wz_r.at[i], {"mp": self.mp_peer(k)})
        for j in range(1, self.nq):
            n = i * (self.nq - 1) + j - 1
            where = {"dp": 2 * self.quarter(j) + self.c}
            self.send(piece, piece, self.r.wp_s.at[n], self.r.wp_r.at[n], where)

    def gather_core(self, m, k):
        w, cols = self.weights[m]
        i = m * 3 + k - 1
        shard = shard_of(self.z, k)
        for j in range(1, self.nq):
            n = i * (self.nq - 1) + j - 1
            got = w.at[shard, self.piece_rows(self.quarter(self.nq - j)), cols]
            where = {"dp": 2 * self.quarter(j) + self.c}
            self.arrive(got, self.r.wp_s.at[n], self.r.wp_r.at[n], where)
        start(self.gather_core_copies(m, k))

    def gather_core_copies(self, m, k):
        w, cols = self.weights[m]
        i = m * 3 + k - 1
        part = w.at[shard_of(self.z, k), self.half(self.c), cols]
        return [remote(part, part, self.r.wc_s.at[i], self.r.wc_r.at[i], {"dp": self.other})]

    def gather_done(self, m, k):
        w, cols = self.weights[m]
        i = m * 3 + k - 1
        part = w.at[shard_of(self.z, k), self.half(1 - self.c), cols]
        self.arrive(part, self.r.wc_s.at[i], self.r.wc_r.at[i], {"dp": self.other})

    def coarse_copies(self, here5, here6, there5, there6, sems):
        a, b = sems
        send = [remote(here5, there5, a.at[0], b.at[0], {"mp": self.near})]
        for j in range(2):
            where = {"mp": self.far + j}
            dst = there6.at[self.par]
            send.append(remote(here6[j], dst, a.at[1 + j], b.at[1 + self.par], where))
        return send

    def coarse_start(self, *args):
        self.coarse = self.coarse_copies(*args)
        start(self.coarse)

    def coarse_arrive(self, there5, there6, sems):
        a, b = sems
        self.arrive(there5, a.at[0], b.at[0], {"mp": self.near})
        for j in range(2):
            self.arrive(there6.at[j], a.at[1 + j], b.at[1 + j], {"mp": self.far + j})

    def coarse_send(self):
        r = self.r
        self.coarse_start(r.out5, (r.out6, r.out6), r.in5, r.in6, (r.cf_s, r.cf_r))

    def coarse_wait(self):
        r = self.r
        self.coarse_arrive(r.in5, r.in6, (r.cf_s, r.cf_r))

    def coarse_clear(self):
        for copy in self.coarse:
            copy.wait_send()

    def coarse_back(self):
        r = self.r
        here = (r.back6.at[0], r.back6.at[1])
        self.coarse_start(r.out5, here, r.near5, r.far6, (r.cb_s, r.cb_r))

    def coarse_back_wait(self):
        r = self.r
        self.coarse_arrive(r.near5, r.far6, (r.cb_s, r.cb_r))

    def norms_z(self):
        r = self.r
        r.nz[self.z] = r.norms[...]
        for k in range(1, NMP):
            dst = r.nz.at[self.z]
            where = {"mp": self.mp_peer(k)}
            self.send(r.norms, dst, r.nz_s.at[k - 1], r.nz_r.at[k - 1], where)

    def norms_dp(self):
        r = self.r
        for k in range(1, NMP):
            got = r.nz.at[self.mp_peer(NMP - k)]
            self.arrive(got, r.nz_s.at[k - 1], r.nz_r.at[k - 1], {"mp": self.mp_peer(k)})
        tot = r.nz[0]
        for k in range(1, NMP):
            tot = tot + r.nz[k]
        r.np[self.me] = tot
        for k in range(1, self.ndp):
            dst = r.np.at[self.me]
            where = {"dp": self.dp_peer(k)}
            self.send(dst, dst, r.np_s.at[k - 1], r.np_r.at[k - 1], where)

    def norms_done(self):
        r = self.r
        for k in range(1, self.ndp):
            got = r.np.at[self.dp_peer(self.ndp - k)]
            self.arrive(got, r.np_s.at[k - 1], r.np_r.at[k - 1], {"dp": self.dp_peer(k)})
        tot = r.np[0]
        for k in range(1, self.ndp):
            tot = tot + r.np[k]
        r.onorm[...] = tot

    def finish(self):
        cores = [c for m in range(4) for k in (1, 2, 3) for c in self.gather_core_copies(m, k)]
        for copy in self.sent + cores:
            copy.wait_send()


def start(copies):
    for copy in copies:
        copy.start()


class Sum:
    def __init__(self, net, r, name):
        self.net = net
        for n in ("g", "rc", "rp", "pz", "rz", "fin", "c_s", "c_r", "p_s", "p_r", "z_s", "z_r", "s_s", "s_r"):
            setattr(self, n, getattr(r, name + "_" + n))
        self.parts = self.g.shape[1]

    def core_copies(self, k):
        net = self.net
        src = self.g.at[k, :, net.half(1 - net.c), :]
        return [remote(src, self.rc.at[k], self.c_s.at[k], self.c_r.at[k], {"dp": net.other})]

    def plane_copies(self, k):
        net, copies = self.net, []
        for j in range(1, net.nq):
            n = k * (net.nq - 1) + j - 1
            to = net.quarter(j)
            src = self.g.at[k, :, net.piece_rows(to), :]
            where = {"dp": 2 * to + net.c}
            copies.append(remote(src, self.rp.at[k, j - 1], self.p_s.at[n], self.p_r.at[n], where))
        return copies

    def z_copies(self, k):
        where = {"mp": shard_of(self.net.z, k)}
        src, dst = self.pz.at[k - 1], self.rz.at[k - 1]
        return [remote(src, dst, self.z_s.at[k - 1], self.z_r.at[k - 1], where)]

    def share_copies(self):
        net, copies = self.net, []
        part = self.fin.at[:, net.rows_of(net.me), :]
        for j in range(1, net.nq):
            where = {"dp": 2 * net.quarter(j) + net.c}
            copies.append(remote(part, part, self.s_s.at[j - 1], self.s_r.at[j - 1], where))
        return copies

    def share_core_copies(self):
        net = self.net
        n = net.nq - 1
        part = self.fin.at[:, net.half(net.c), :]
        return [remote(part, part, self.s_s.at[n], self.s_r.at[n], {"dp": net.other})]

    def core(self, k):
        start(self.core_copies(k))

    def plane(self, k):
        net = self.net
        net.arrive(self.rc.at[k], self.c_s.at[k], self.c_r.at[k], {"dp": net.other})

        def add(i):
            a, b = i // 2, lax.rem(i, 2)
            rows = pl.ds(pl.multiple_of(net.c * HALF + b * 128, 128), 128)
            more = self.rc[k, a, rows_at(b, 128), :].astype(f32)
            self.g[k, a, rows, :] = (self.g[k, a, rows, :].astype(f32) + more).astype(bf16)

        loop(2 * self.parts, add)
        start(self.plane_copies(k))

    def total(self, k):
        net = self.net
        for j in range(1, net.nq):
            n = k * (net.nq - 1) + j - 1
            where = {"dp": 2 * net.quarter(j) + net.c}
            net.arrive(self.rp.at[k, j - 1], self.p_s.at[n], self.p_r.at[n], where)
        tots = []
        for a in range(self.parts):
            tot = self.g[k, a, net.piece_rows(net.q), :].astype(f32)
            for j in range(net.nq - 1):
                tot = tot + self.rp[k, j, a].astype(f32)
            tots.append(tot)
        return tots

    def pass_on(self, k):
        for a, tot in enumerate(self.total(k)):
            self.pz[k - 1, a] = tot.astype(bf16)
        start(self.z_copies(k))

    def share(self):
        net = self.net
        tots = self.total(0)
        for k in range(1, NMP):
            where = {"mp": shard_of(net.z, k)}
            net.arrive(self.rz.at[k - 1], self.z_s.at[k - 1], self.z_r.at[k - 1], where)
            tots = [tot + self.rz[k - 1, a].astype(f32) for a, tot in enumerate(tots)]
        mine = net.rows_of(net.me)
        for a, tot in enumerate(tots):
            self.fin[a, mine, :] = tot.astype(bf16)
        start(self.share_copies())

    def share_core(self):
        net = self.net
        for j in range(1, net.nq):
            got = self.fin.at[:, net.piece_rows(net.quarter(net.nq - j)), :]
            where = {"dp": 2 * net.quarter(j) + net.c}
            net.arrive(got, self.s_s.at[j - 1], self.s_r.at[j - 1], where)
        start(self.share_core_copies())

    def done(self):
        net = self.net
        n = net.nq - 1
        part = self.fin.at[:, net.half(1 - net.c), :]
        net.arrive(part, self.s_s.at[n], self.s_r.at[n], {"dp": net.other})

    def finish(self):
        def step(k):
            for copy in self.core_copies(k) + self.plane_copies(k):
                copy.wait_send()

        loop(NMP, step)
        last = [copy for k in range(1, NMP) for copy in self.z_copies(k)]
        for copy in last + self.share_copies() + self.share_core_copies():
            copy.wait_send()


def whole_kernel(ndp, r):
    net = Links(r, ndp)
    z = net.z
    r.gq, r.gk, r.gv = (e.at[pl.ds(0, T), :] for e in (r.qe, r.ke, r.ve))
    net.weights = (
        (r.wat, pl.ds(0, 384)),
        (r.wup, pl.ds(0, 512)),
        (r.wdn, pl.ds(0, 512)),
        (r.wat, pl.ds(384, 128)),
    )
    r.mx, r.gof = r.h2, r.pool
    r.fa, r.fb = r.tops, r.sumz
    net_f, net_o, net_a = (Sum(net, r, n) for n in "foa")
    shard = [shard_of(z, k) for k in range(NMP)]
    loads = [pltpu.make_async_copy(r.x_in, r.raw, r.ld.at[0])]
    for i, w in enumerate((r.w_query, r.w_key, r.w_value)):
        dst = r.wat.at[z, :, pl.ds(i * 128, 128)]
        loads.append(pltpu.make_async_copy(w, dst, r.ld.at[1 + i]))
    loads.append(pltpu.make_async_copy(r.w_up, r.wup.at[z], r.ld.at[4]))
    loads.append(pltpu.make_async_copy(r.w_down, r.wdn.at[z], r.ld.at[5]))
    start(loads)
    net.greet()
    loads[0].wait()
    by_document(r.x, r.raw)
    load_gy = pltpu.make_async_copy(r.gy_in, r.raw, r.ld.at[6])
    load_gy.start()
    norm_one(r)
    r.wat[z, :, pl.ds(384, 128)] = r.w_output[...].T
    for copy in loads[1:4]:
        copy.wait()
    net.barrier()
    for m in (0, 3):
        for k in (1, 2, 3):
            net.gather_z(m, k)
    for copy in loads[4:]:
        copy.wait()
    build_tables(r, z, 0)
    build_tables(r, z, 1)
    for m in (0, 3):
        for k in (1, 2, 3):
            net.gather_plane(m, k)
    for k in (1, 2, 3):
        net.gather_z(1, k)
        net.gather_z(2, k)
    build_maps(r)
    project(r, z, shard[:1])
    pool_levels(r, shard[:1])
    for k in (1, 2, 3):
        net.gather_core(0, k)
    attend_own(r, shard[0])
    for m in (1, 2):
        net.gather_plane(m, 1)
    for k in (1, 2, 3):
        net.gather_done(0, k)
    project(r, z, shard[1:])
    for k in (1, 2, 3):
        net.gather_core(3, k)
    for m in (1, 2):
        net.gather_plane(m, 2)
    pool_levels(r, shard[1:])
    net.coarse_send()
    for m in (1, 2):
        net.gather_plane(m, 3)
    for c in range(7):
        attend_chunk(r, c, shard[1:])
    net.coarse_wait()
    net.coarse_clear()
    place_remote(r)
    attend_chunk(r, EXT // 128 - 1, range(NMP))
    combine_sums(r)
    load_gy.wait()
    by_document(r.gy, r.raw)
    combine_values(r)
    for k in (1, 2, 3):
        net.gather_done(3, k)
    attn_out(r)

    def ffn_step(k):
        f = shard_of(z, k)

        @pl.when(k > 0)
        def _():
            net.gather_done(1, k)
            net.gather_done(2, k)

        ffn_inner(r, f)

        @pl.when(k < NMP - 1)
        def _():
            net.gather_core(1, k + 1)
            net.gather_core(2, k + 1)

        ffn_grads(r, f, k)
        net_f.core(k)

        @pl.when(k > 0)
        def _():
            net_f.plane(k - 1)

    loop(NMP, ffn_step)
    ffn_outer(r, 0)
    net_f.plane(3)
    ffn_outer(r, 1)
    put_mixed = pltpu.make_async_copy(r.mx, r.mixed, r.st.at[0])
    put_mixed.start()
    out_grads(r, z)
    for k in range(NMP):
        net_o.core(k)
    net_f.pass_on(1)
    context_grads(r)
    attn_back_rows(r)
    for k in range(NMP):
        net_o.plane(k)
    attend_back_chunk(r, EXT // 128 - 1, False, range(NMP))
    for s in range(NMP):
        values_back(r, 7, s)
    save_remote(r)
    net.coarse_back()
    net_f.pass_on(2)

    def back_step(i):
        k = lax.rem(i + 1, NMP)
        s = shard_of(z, k)
        attend_back_pair(r, s)

        @pl.when(i == 0)
        def _():
            net.coarse_back_wait()

        unpool(r, z, s)

        @pl.when(i > 0)
        def _():
            net_a.plane(i)

        attn_grads(r, s, k)
        net_a.core(k)

        @pl.when(i == 0)
        def _():
            net_f.pass_on(3)
            for n in range(1, NMP):
                net_o.pass_on(n)

        @pl.when(i == 1)
        def _():
            net_f.share()

        @pl.when(i == 2)
        def _():
            net_o.share()
            net_f.share_core()

        @pl.when(i > 1)
        def _():
            net_a.pass_on(i - 1)

    loop(NMP, back_step)
    input_grads(r, 0)
    net_a.plane(0)
    net_o.share_core()
    input_grads(r, 1)
    net_a.pass_on(3)
    net.norms_z()
    put_gx = pltpu.make_async_copy(r.gxs, r.gx, r.st.at[1])
    put_gx.start()
    net_f.done()
    net_o.done()
    stores = [put_mixed, put_gx]
    for i, (a, b) in enumerate(((r.f_fin, r.ofn), (r.o_fin, r.oot), (r.a_fin, r.oat))):
        stores.append(pltpu.make_async_copy(a, b, r.st.at[2 + i]))
    start(stores[2:4])
    net_a.share()
    net.norms_dp()
    net_a.share_core()
    net.norms_done()
    net_a.done()
    start(stores[4:])
    for copy in stores:
        copy.wait()
    net.coarse_clear()
    net.finish()
    for each in (net_f, net_o, net_a):
        each.finish()


FAR_OUTS = ("mixed", "gx", "ofn", "oot", "oat")


def run(body, ins, outs, scratch, sems):
    names = list(ins) + list(outs) + list(scratch) + list(sems)

    def kernel(*refs):
        body(types.SimpleNamespace(**dict(zip(names, refs))))

    result = pl.pallas_call(
        kernel,
        out_shape=[jax.ShapeDtypeStruct(*v) for v in outs.values()],
        in_specs=[pl.BlockSpec(memory_space=space) for _, space in ins.values()],
        out_specs=[
            pl.BlockSpec(memory_space=pl.ANY if n in FAR_OUTS else pltpu.VMEM) for n in outs
        ],
        scratch_shapes=[pltpu.VMEM(*v) for v in scratch.values()]
        + [pltpu.SemaphoreType.DMA((n,)) for n in sems.values()],
        compiler_params=pltpu.CompilerParams(
            vmem_limit_bytes=63 * 1024 * 1024, collective_id=0, has_side_effects=True
        ),
    )(*[a for a, _ in ins.values()])
    return dict(zip(outs, result))


def per_device(
    ndp,
    tokens,
    lengths,
    gain_one,
    shift_one,
    w_query,
    w_key,
    w_value,
    w_output,
    gain_two,
    shift_two,
    w_up,
    w_down,
    cotangent,
):
    g1, b1, g2, b2 = (v.reshape(1, D) for v in (gain_one, shift_one, gain_two, shift_two))
    nq, piece = ndp // 2, LOC // ndp
    vmem, any_space = pltpu.VMEM, pl.ANY
    ins = dict(
        lens=(lengths, pltpu.SMEM),
        x_in=(tokens, any_space),
        gy_in=(cotangent, any_space),
        g1=(g1, vmem),
        b1=(b1, vmem),
        g2=(g2, vmem),
        b2=(b2, vmem),
        w_query=(w_query, any_space),
        w_key=(w_key, any_space),
        w_value=(w_value, any_space),
        w_output=(w_output, vmem),
        w_up=(w_up, any_space),
        w_down=(w_down, any_space),
    )
    outs = dict(
        mixed=((T, D), bf16),
        gx=((T, D), f32),
        ofn=((2, D, 512), bf16),
        oot=((1, D, 128), bf16),
        oat=((1, D, 384), bf16),
        onorm=((8, D), f32),
    )
    scratch = dict(
        x=((T, D), bf16),
        gy=((T, D), bf16),
        gxs=((T, D), f32),
        inv=((ND + 1, EXT - LOC, 128), f32),
        wat=((NMP, D, 512), bf16),
        wup=((NMP, D, 512), bf16),
        wdn=((NMP, 512, D), bf16),
        h1=((T, D), bf16),
        qe=((ND * EXT, D), bf16),
        ke=((ND * EXT, D), bf16),
        ve=((ND * EXT, D), bf16),
        pool=((EXT - LOC, LOC), bf16),
        unpool=((LOC, EXT - LOC), bf16),
        cc=((ND * EXT, 128), bf16),
        bias=((ND * EXT, 128), bf16),
        wts=((64 * 128, 256), bf16),
        num=((ND * EXT, D), f32),
        tops=((EXT, 128), f32),
        sumz=((EXT, 128), f32),
        up=((LOC, 128), f32),
        up2=((LOC, 128), f32),
        ctx=((T, D), bf16),
        h2=((T, D), bf16),
        act=((T, FF), bf16),
        gp=((T, FF), bf16),
        gm=((T, D), bf16),
        hc=((T // 2, D), f32),
        dl=((EXT, 128), f32),
        ee=((ND, 256, D), bf16),
        crow=((ND * EXT // 128, 128), f32),
        raw=((LOC, ND, D), bf16),
        out5=((2 * ND, 16, D), bf16),
        out6=((ND, 16, D), bf16),
        in5=((2 * ND, 16, D), bf16),
        in6=((2, ND, 16, D), bf16),
        back6=((2, ND, 16, D), bf16),
        near5=((2 * ND, 16, D), bf16),
        far6=((2, ND, 16, D), bf16),
        norms=((8, D), f32),
        nz=((NMP, 8, D), f32),
        np=((ndp, 8, D), f32),
    )
    counts = dict(wz=12, wp=12 * (nq - 1), wc=12, cf=3, cb=3, nz=3, np=ndp - 1)
    for n, a, cols in (("f", 2, 512), ("o", 1, 128), ("a", 1, 384)):
        scratch[n + "_g"] = ((NMP, a, 512, cols), bf16)
        scratch[n + "_rc"] = ((NMP, a, HALF, cols), bf16)
        scratch[n + "_rp"] = ((NMP, nq - 1, a, piece, cols), bf16)
        scratch[n + "_pz"] = ((NMP - 1, a, piece, cols), bf16)
        scratch[n + "_rz"] = ((NMP - 1, a, piece, cols), bf16)
        scratch[n + "_fin"] = ((a, 512, cols), bf16)
        counts.update({n + "_c": NMP, n + "_p": NMP * (nq - 1), n + "_z": NMP - 1, n + "_s": nq})
    sems = dict(ld=7, st=5)
    for n, count in counts.items():
        sems[n + "_s"] = count
        sems[n + "_r"] = count
    o = run(lambda r: whole_kernel(ndp, r), ins, outs, scratch, sems)

    outs = emit(o)
    return (*outs, *(o["onorm"][i] for i in range(4)))


def emit_kernel(mixed, gx, fn, at, ot, o_mixed, o_gx, o_q, o_k, o_v, o_o, o_up, o_dn):
    for d in range(ND):
        o_mixed[:, d, :] = mixed[d]
        o_gx[:, d, :] = gx[d]
    for i, out in enumerate((o_q, o_k, o_v)):
        out[...] = at[0, :, i * 128 : (i + 1) * 128].astype(f32)
    o_up[...] = fn[0].astype(f32)
    o_dn[...] = fn[1].astype(f32)
    o_o[...] = ot[0].astype(f32).T


def emit(o):
    n = 4
    rows = LOC // n

    def tiles(*shape, axis):
        block = tuple(rows if i == axis else size for i, size in enumerate(shape))
        return pl.BlockSpec(block, lambda i: tuple(i if a == axis else 0 for a in range(len(shape))))

    doc = tiles(ND, LOC, D, axis=1)
    pos = tiles(LOC, ND, D, axis=0)
    third, whole = tiles(512, 128, axis=0), tiles(512, D, axis=0)
    shape = jax.ShapeDtypeStruct
    return pl.pallas_call(
        emit_kernel,
        grid=(n,),
        in_specs=[
            doc,
            doc,
            tiles(2, 512, 512, axis=1),
            tiles(1, 512, 384, axis=1),
            tiles(1, 512, 128, axis=1),
        ],
        out_specs=[pos, pos, third, third, third, tiles(128, D, axis=1), whole, whole],
        out_shape=[shape((LOC, ND, D), bf16), shape((LOC, ND, D), f32)]
        + [shape((D, 128), f32)] * 3
        + [shape((128, D), f32), shape((D, 512), f32), shape((512, D), f32)],
    )(o["mixed"].reshape(ND, LOC, D), o["gx"].reshape(ND, LOC, D), o["ofn"], o["oat"], o["oot"])


def solution(mesh):
    tok = P("mp", "dp", None)
    col, row, rep = P(None, "mp"), P("mp", None), P()
    ndp = mesh.shape["dp"]
    return jax.shard_map(
        lambda *args: per_device(ndp, *args),
        mesh=mesh,
        in_specs=(tok, P("dp"), rep, rep, col, col, col, row, rep, rep, col, row, tok),
        out_specs=(tok, tok, col, col, col, row, col, row, rep, rep, rep, rep),
        check_vma=False,
    )
```

```python
import types

import jax
import jax.numpy as jnp
from jax import lax
from jax.experimental import pallas as pl
from jax.experimental.pallas import tpu as pltpu
from jax.sharding import PartitionSpec as P

HD = 64
BLK = 16
NEG = -1e30
FLOOR = -1e29
EPS = 1e-05
LOC = 512
ND = 2
D = 512
FF = 2048
NMP = 4
HALF = 256
T = ND * LOC
HEADS = D // HD
LEVELS = 7
LOCAL_LEVELS = 5
EXT = 1024
RT = 512
G = [LOC >> lev for lev in range(LEVELS)]
OFF = [sum(G[:lev]) for lev in range(LEVELS)]
bf16 = jnp.bfloat16
f32 = jnp.float32
i32 = jnp.int32


def dot(a, b, ca=1, cb=0):
    return lax.dot_general(a, b, (((ca,), (cb,)), ((), ())), preferred_element_type=f32)


def iota(shape, axis):
    return lax.broadcasted_iota(i32, shape, axis)


def loop(n, body):
    lax.fori_loop(0, n, lambda i, c: (body(i), c)[1], 0)


def rows_at(i, size):
    return pl.ds(pl.multiple_of(i * size, size), size)


def own_groups(e):
    size = jnp.zeros_like(e)
    start = jnp.zeros_like(e)
    for lev in range(LEVELS):
        here = (e >= OFF[lev]) & (e < OFF[lev] + G[lev])
        size = jnp.where(here, 1 << lev, size)
        start = jnp.where(here, (e - OFF[lev]) << lev, start)
    return size, start


def key_groups(e, z):
    size, start = own_groups(e)
    start = start + z * LOC
    near = z + 1 - 2 * lax.rem(z, 2)
    far = 1 - z // 2
    size = jnp.where(e >= OFF[5], 32, size)
    start = jnp.where(e >= OFF[5], near * LOC + (e - OFF[5]) * 32, start)
    size = jnp.where(e >= OFF[6], 64, size)
    start = jnp.where(e >= OFF[6], far * 2 * LOC + (e - OFF[6]) * 64, start)
    return size, start


def count_live(size, start, length):
    return jnp.clip(length - start, 0, size).astype(f32)


def build_tables(r, z, d):
    r.ee[d] = head_map(d)
    length = r.lens[d]
    inv, inv_size = inv_counts(r, z, d)
    r.inv[d] = inv
    r.inv[ND] = inv_size

    def chunk(c):
        at = pl.ds(pl.multiple_of(d * EXT + c * 128, 128), 128)
        e_col = iota((128, 128), 0) + c * 128
        size, start = key_groups(e_col, z)
        r.cc[at, :] = count_live(size, start, length).astype(bf16)
        e_row = iota((1, 128), 1) + c * 128
        size, start = key_groups(e_row, z)
        dead = count_live(size, start, length)
        r.crow[pl.ds(d * (EXT // 128) + c, 1), :] = dead
        q_blk, k_blk = e_col // BLK, jnp.broadcast_to(e_row // BLK, (128, 128))
        span = jnp.where(q_blk // 2 == k_blk // 2, 0.0, NEG)
        same = jnp.where(q_blk == k_blk, 0.0, NEG)
        cross = jnp.where(q_blk == k_blk, NEG, span)
        bias = jnp.where(e_col < LOC, span, jnp.where(e_col < OFF[5], cross, same))
        r.bias[at, :] = jnp.where(jnp.broadcast_to(dead, (128, 128)) > 0.0, bias, NEG).astype(bf16)

    loop(EXT // 128, chunk)


def build_maps(r):
    def tile(c):
        rows = rows_at(c, 128)
        size, start = own_groups(iota((128, LOC), 0) + c * 128 + LOC)
        pos = iota((128, LOC), 1)
        r.pool[rows, :] = ((pos >= start) & (pos < start + size)).astype(f32).astype(bf16)
        size, start = own_groups(iota((128, EXT - LOC), 1) + LOC)
        pos = iota((128, EXT - LOC), 0) + c * 128
        r.unpool[rows, :] = ((pos >= start) & (pos < start + size)).astype(f32).astype(bf16)

    loop((EXT - LOC) // 128, tile)


def inv_counts(r, z, d):
    e = iota((EXT - LOC, 128), 0) + LOC
    size, start = own_groups(e)
    cnt = count_live(size, start + z * LOC, r.lens[d])
    return 1.0 / jnp.maximum(cnt, 1.0), 1.0 / jnp.maximum(size, 1).astype(f32)


def wide(col):
    return jnp.concatenate([col] * (D // 128), axis=1)


def live_rows(r, z, d, first, count):
    pos = iota((count, D), 0) + first + z * LOC
    return pos < r.lens[d]


def stats(v):
    mean = jnp.mean(v, axis=-1, keepdims=True)
    cen = v - mean
    var = jnp.mean(cen * cen, axis=-1, keepdims=True)
    return cen, lax.rsqrt(var + EPS)


def by_document(dst, raw):
    def tile(t):
        v = raw[rows_at(t, 128)].astype(f32)
        for d in range(ND):
            at = pl.ds(pl.multiple_of(d * LOC + t * 128, 128), 128)
            dst[at, :] = v[:, d, :].astype(bf16)

    loop(LOC // 128, tile)


def norm_one(r):
    r.tops[...] = jnp.zeros_like(r.tops)
    r.sumz[...] = jnp.zeros_like(r.sumz)
    r.norms[...] = jnp.zeros_like(r.norms)

    def tile(t):
        rows = rows_at(t, RT)
        cen, rstd = stats(r.x[rows, :].astype(f32))
        r.h1[rows, :] = (cen * rstd * r.g1[...] + r.b1[...]).astype(bf16)

    loop(T // RT, tile)


def ext_rows(d, off, count):
    return pl.ds(d * EXT + off, count)


def attn_weight(r, t):
    return jnp.concatenate([r.wat[s, :, t * 128 : (t + 1) * 128] for s in range(NMP)], axis=1)


def pair_lanes(s):
    return pl.ds(pl.multiple_of(s * 128, 128), 128)


def project(r, z, shards):
    for d in range(ND):

        def tile(t, d=d):
            rows = pl.ds(pl.multiple_of(d * LOC + t * RT, RT), RT)
            at = pl.ds(pl.multiple_of(d * EXT + t * RT, RT), RT)
            w = [r.wat[s, :, 0:384] for s in shards]
            o = dot(r.h1[rows, :], jnp.concatenate(w, axis=1))
            live = iota((RT, 128), 0) + t * RT + z * LOC < r.lens[d]
            for i, s in enumerate(shards):
                lanes = pair_lanes(s)
                q, k, v = (o[:, i * 384 + j * 128 : i * 384 + (j + 1) * 128] for j in range(3))
                r.qe[at, lanes] = (q.astype(bf16).astype(f32) * (HD**-0.5)).astype(bf16)
                r.ke[at, lanes] = jnp.where(live, k, 0.0).astype(bf16)
                r.ve[at, lanes] = jnp.where(live, v, 0.0).astype(bf16)

        loop(LOC // RT, tile)


def pool_levels(r, shards):
    keep = OFF[5] - LOC
    for d in range(ND):
        fine = ext_rows(d, 0, LOC)
        x = [e[fine, pair_lanes(s)] for s in shards for e in (r.qe, r.ke, r.ve)]
        o = dot(r.pool[...], jnp.concatenate(x, axis=1))
        for i, s in enumerate(shards):
            lanes = pair_lanes(s)
            q, k, v = (o[:, i * 384 + j * 128 : i * 384 + (j + 1) * 128] for j in range(3))
            r.qe[ext_rows(d, LOC, LOC), lanes] = (q * r.inv[ND]).astype(bf16)
            k = k * r.inv[d]
            r.ke[ext_rows(d, LOC, keep), lanes] = k[:keep].astype(bf16)
            r.ve[ext_rows(d, LOC, keep), lanes] = v[:keep].astype(bf16)
            r.out5[2 * d, :, lanes] = k[keep : keep + 16].astype(bf16)
            r.out5[2 * d + 1, :, lanes] = v[keep : keep + 16].astype(bf16)
            last = [k[keep + 16 : keep + 24], v[keep + 16 : keep + 24]]
            r.out6[d, :, lanes] = jnp.concatenate(last, axis=0).astype(bf16)


def place_remote(r):
    for d in range(ND):
        for kv, e in enumerate((r.ke, r.ve)):
            far = [r.in6[j, d].astype(f32)[kv * 8 : kv * 8 + 8] for j in range(2)]
            e[ext_rows(d, OFF[5], 16), :] = r.in5[2 * d + kv]
            e[ext_rows(d, OFF[6], 16), :] = jnp.concatenate(far, axis=0).astype(bf16)


def split_heads(pair):
    first = iota(pair.shape, 1) < HD
    zero = jnp.zeros_like(pair)
    return jnp.concatenate([jnp.where(first, pair, zero), jnp.where(first, zero, pair)], axis=0)


def count_lanes(cc, d, p):
    lane = iota(cc.shape, 1)
    zero = jnp.zeros_like(cc)
    a = jnp.where(lane == d * HEADS + 2 * p, cc, zero)
    b = jnp.where(lane == d * HEADS + 2 * p + 1, cc, zero)
    return jnp.concatenate([a, b], axis=0)


def attend_step(r, c, d, s, tops, sums):
    lane = iota((128, 128), 1)
    at = pl.ds(pl.multiple_of(d * EXT + c * 128, 128), 128)
    bias = r.bias[at, :].astype(f32)
    lanes = pair_lanes(s)
    w = dot(r.qe[at, lanes], split_heads(r.ke[at, lanes]), 1, 1)
    parts = []
    for j in range(2):
        sj = w[:, j * 128 : (j + 1) * 128] + bias
        top = jnp.maximum(jnp.max(sj, axis=1, keepdims=True), FLOOR)
        parts.append(jnp.exp(sj - top))
        tops = jnp.where(lane == d * HEADS + 2 * s + j, top, tops)
    e = jnp.concatenate(parts, axis=1).astype(bf16)
    r.wts[pl.ds(pl.multiple_of(((c * ND + d) * 4 + s) * 128, 128), 128), :] = e
    cnt = count_lanes(r.cc[at, :], d, s)
    o = dot(e, jnp.concatenate([split_heads(r.ve[at, lanes]), cnt], axis=1))
    r.num[at, lanes] = o[:, :128]
    return tops, sums + o[:, 128:]


def attend_chunk(r, c, pairs):
    here = rows_at(c, 128)
    tops, sums = r.tops[here, :], r.sumz[here, :]
    for s in pairs:
        for d in range(ND):
            tops, sums = attend_step(r, c, d, s, tops, sums)
    r.tops[here, :] = tops
    r.sumz[here, :] = sums


def attend_own(r, s):
    def two(i):
        attend_chunk(r, 2 * i, (s,))
        attend_chunk(r, 2 * i + 1, (s,))

    loop(3, two)
    attend_chunk(r, 6, (s,))


def combine_sums(r):
    last = pl.ds(OFF[6], G[6])
    top = r.tops[last, :]
    tot = r.sumz[last, :]
    for lev in range(LEVELS - 2, -1, -1):
        n = G[lev]
        for half in range(2):
            r.up[pl.ds(half, n // 2, stride=2), :] = top
            r.up2[pl.ds(half, n // 2, stride=2), :] = tot
        at = pl.ds(OFF[lev], n)
        up_top = r.up[pl.ds(0, n), :]
        own = r.tops[at, :]
        top = jnp.maximum(own, up_top)
        a = jnp.exp(own - top)
        b = jnp.exp(up_top - top)
        tot = a * r.sumz[at, :] + b * r.up2[pl.ds(0, n), :]
        if lev == 0:
            used = iota(tot.shape, 1) < ND * HEADS
            inv = 1.0 / jnp.where(used, tot, 1.0)
            a, b = a * inv, b * inv
        r.fa[at, :] = a
        r.fb[at, :] = b


def high_low(v, axis):
    hi = v.astype(bf16).astype(f32)
    return jnp.concatenate([hi, v - hi], axis=axis).astype(bf16)


def spread(r, fac, d):
    return dot(high_low(fac, 1), r.ee[d])


def head_map(d):
    row = lax.rem(iota((256, D), 0), 128)
    return (row == d * HEADS + iota((256, D), 1) // HD).astype(f32).astype(bf16)


def up_map(n):
    return (iota((n, n), 0) // 2 == lax.rem(iota((n, n), 1), n // 2)).astype(f32).astype(bf16)


def down_map(n):
    return (lax.rem(iota((2 * n, n // 2), 0), n) // 2 == iota((2 * n, n // 2), 1)).astype(f32).astype(bf16)


def combine_values(r):
    for d in range(ND):
        cur = r.num[ext_rows(d, OFF[6], G[6]), :]
        for lev in range(LEVELS - 2, -1, -1):
            n = G[lev]
            parts = []
            step = min(n, 256)
            for t in range(n // step):
                at = pl.ds(OFF[lev] + t * step, step)
                here = ext_rows(d, OFF[lev] + t * step, step)
                fac = spread(r, jnp.concatenate([r.fa[at, :], r.fb[at, :]], axis=0), d)
                up = dot(up_map(step), high_low(cur[t * step // 2 : (t + 1) * step // 2], 0))
                parts.append(fac[:step] * r.num[here, :] + fac[step:] * up)
                if lev == 0:
                    r.ctx[pl.ds(d * LOC + t * step, step), :] = parts[-1].astype(bf16)
                    r.num[here, :] = parts[-1]
            cur = jnp.concatenate(parts, axis=0) if len(parts) > 1 else parts[0]


def spare_rows(t):
    per = LOC // RT
    return pl.ds(pl.multiple_of((t // per) * EXT + LOC + lax.rem(t, per) * RT, RT), RT)


def attn_out(r):
    def tile(t):
        rows = rows_at(t, RT)
        mid = r.x[rows, :].astype(f32) + dot(r.ctx[rows, :], attn_weight(r, 3), 1, 1)
        r.num[spare_rows(t), :] = mid
        cen, rstd = stats(mid)
        r.h2[rows, :] = (cen * rstd * r.g2[...] + r.b2[...]).astype(bf16)

    loop(T // RT, tile)


def ffn_inner(r, f):
    cols = rows_at(f, 512)
    n = 256
    for t in range(T // n):
        rows = pl.ds(t * n, n)
        pre = dot(r.h2[rows, :], r.wup[f])
        ga = dot(r.gy[rows, :], r.wdn[f], 1, 1)
        cdf = 0.5 + 0.5 * lax.erf(pre * (0.5**0.5))
        r.act[rows, cols] = (pre * cdf).astype(bf16)
        pdf = jnp.exp(pre * pre * -0.5) * 0.3989422804014327
        r.gp[rows, cols] = (ga * (cdf + pre * pdf)).astype(bf16)


def ffn_grads(r, f, k):
    cols = rows_at(f, 512)
    r.f_g[k, 0] = dot(r.h2[...], r.gp[:, cols], 0, 0).astype(bf16)
    r.f_g[k, 1] = dot(r.act[:, cols], r.gy[...], 0, 0).astype(bf16)


def norm_back(v, gain, gh, r, row):
    cen, rstd = stats(v)
    xhat = cen * rstd
    r.norms[row : row + 1, :] += jnp.sum(gh * xhat, axis=0, keepdims=True)
    r.norms[row + 1 : row + 2, :] += jnp.sum(gh, axis=0, keepdims=True)
    u = gh * gain
    return rstd * (
        u - jnp.mean(u, axis=-1, keepdims=True) - xhat * jnp.mean(u * xhat, axis=-1, keepdims=True)
    )


def ffn_outer(r, t):
    rows = rows_at(t, RT)
    mid = r.num[spare_rows(t), :]
    ffn = dot(r.act[rows, 0:512], r.wdn[0])
    gh2 = dot(r.gp[rows, 0:512], r.wup[0], 1, 1)
    for f in range(1, NMP):
        cols = slice(f * 512, (f + 1) * 512)
        ffn = ffn + dot(r.act[rows, cols], r.wdn[f])
        gh2 = gh2 + dot(r.gp[rows, cols], r.wup[f], 1, 1)
    r.mx[rows, :] = (mid + ffn).astype(bf16)
    g_mid = r.gy[rows, :].astype(f32) + norm_back(mid, r.g2[...], gh2, r, 2)
    r.gxs[rows, :] = g_mid
    r.gm[rows, :] = g_mid.astype(bf16)


def out_grads(r, z):
    r.gof[...] = dot(r.gm[...], r.ctx[...], 0, 0).astype(bf16)
    for k in range(NMP):
        r.o_g[k, 0] = r.gof[:, pair_lanes(shard_of(z, k))]


def at_lanes(base, s):
    return pl.ds(pl.multiple_of(base + s * 128, 128), 128)


def store_pair(r, d, off, count, v):
    hi = v.astype(bf16)
    r.act[pl.ds(off, count), d * D : (d + 1) * D] = hi
    r.act[pl.ds(off, count), (ND + d) * D : (ND + d + 1) * D] = (v - hi.astype(f32)).astype(bf16)


def context_grads(r):
    def tile(t):
        r.num[spare_rows(t), :] = dot(r.gm[rows_at(t, RT), :], attn_weight(r, 3))

    loop(T // RT, tile)


def attn_back_rows(r):
    lane_head = lax.rem(iota((2 * D, 128), 0), D) // HD
    n = 256
    for t in range(LOC // n):
        at = pl.ds(t * n, n)
        delta = jnp.zeros((n, 128), f32)
        for d in range(ND):
            gctx = r.num[ext_rows(d, LOC + t * n, n), :]
            sel = (lane_head + d * HEADS == iota((2 * D, 128), 1)).astype(f32).astype(bf16)
            delta = delta + dot(high_low(gctx * r.num[ext_rows(d, t * n, n), :], 1), sel)
            fac = spread(r, jnp.concatenate([r.fa[at, :], r.fb[at, :]], axis=0), d)
            store_pair(r, d, t * n, n, fac[:n] * gctx)
            down = high_low(fac[n:] * gctx, 0)
            r.hc[pl.ds((d * LOC + t * n) // 2, n // 2), :] = dot(down_map(n), down, 0, 0)
        r.dl[at, :] = r.fa[at, :] * delta
        r.up[at, :] = r.fb[at, :] * delta
    acc = r.up[pl.ds(0, LOC // 2, stride=2), :] + r.up[pl.ds(1, LOC // 2, stride=2), :]
    for lev in range(1, LEVELS - 1):
        n = G[lev]
        at = pl.ds(OFF[lev], n)
        r.dl[at, :] = r.fa[at, :] * acc
        r.up[pl.ds(0, n), :] = r.fb[at, :] * acc
        acc = r.up[pl.ds(0, n // 2, stride=2), :] + r.up[pl.ds(1, n // 2, stride=2), :]
    r.dl[pl.ds(OFF[6], 2 * G[6]), :] = jnp.concatenate([acc, jnp.zeros_like(acc)], 0)
    for d in range(ND):
        cur = r.hc[pl.ds(d * LOC // 2, LOC // 2), :]
        for lev in range(1, LEVELS - 1):
            n = G[lev]
            parts = []
            step = min(n, 256)
            for t in range(n // step):
                at = pl.ds(OFF[lev] + t * step, step)
                seg = cur[t * step : (t + 1) * step]
                fac = spread(r, jnp.concatenate([r.fa[at, :], r.fb[at, :]], axis=0), d)
                store_pair(r, d, OFF[lev] + t * step, step, fac[:step] * seg)
                down = high_low(fac[step:] * seg, 0)
                parts.append(dot(down_map(step), down, 0, 0))
            cur = jnp.concatenate(parts, axis=0) if len(parts) > 1 else parts[0]
        store_pair(r, d, OFF[6], 2 * G[6], jnp.concatenate([cur, jnp.zeros_like(cur)], axis=0))


def attend_back_step(r, c, fine, s, d):
    top = iota((128, 128), 0) < HD
    lane = iota((128, 128), 1)
    lanes = pair_lanes(s)
    rows = rows_at(c, 128)
    dl = r.dl[rows, :]
    at = pl.ds(pl.multiple_of(d * EXT + c * 128, 128), 128)
    cnt = jnp.broadcast_to(r.crow[pl.ds(d * (EXT // 128) + c, 1), :], (128, 128))
    g = r.act[rows, at_lanes(d * D, s)]
    low = r.act[rows, at_lanes((ND + d) * D, s)]
    q = r.qe[at, lanes]
    kcat = split_heads(r.ke[at, lanes])
    vcat = split_heads(r.ve[at, lanes])
    dp = dot(jnp.concatenate([g, low], axis=1), jnp.concatenate([vcat, vcat], axis=1), 1, 1)
    e = r.wts[pl.ds(pl.multiple_of(((c * ND + d) * 4 + s) * 128, 128), 128), :]
    parts = []
    for j in range(2):
        half = slice(j * 128, (j + 1) * 128)
        mine = jnp.where(lane == d * HEADS + 2 * s + j, dl, 0.0)
        delta = jnp.sum(mine, axis=1, keepdims=True)
        parts.append(e[:, half].astype(f32) * (dp[:, half] - delta * cnt))
    ds = jnp.concatenate(parts, axis=1).astype(bf16)
    dq = dot(ds, kcat)
    dk = dot(q, ds, 0, 0)
    dk = jnp.where(top, dk[:, :128], dk[:, 128:]).T
    if fine:
        r.num[at, lanes] = dq
        r.num[pl.ds(pl.multiple_of(d * EXT + LOC + c * 128, 128), 128), lanes] = dk
    else:
        coarse = at_lanes((ND + d) * D, s)
        r.gp[rows_at(c - LOC // 128, 128), coarse] = dq.astype(bf16)
        r.gp[rows_at(c, 128), coarse] = dk.astype(bf16)


def attend_back_chunk(r, c, fine, pairs):
    for s in pairs:
        for d in range(ND):
            attend_back_step(r, c, fine, s, d)


def values_back(r, c, s):
    top = iota((128, 128), 0) < HD
    rows = rows_at(c, 128)
    for d in range(ND):
        g = r.act[rows, at_lanes(d * D, s)]
        slot = pl.ds(pl.multiple_of(((c * ND + d) * 4 + s) * 128, 128), 128)
        dv = dot(g, r.wts[slot, :], 0, 0)
        r.gp[rows, at_lanes(d * D, s)] = jnp.where(top, dv[:, :128], dv[:, 128:]).T.astype(bf16)


def attend_back_pair(r, s):
    for c in range(4):
        attend_back_chunk(r, c, True, (s,))
    for c in range(4, 7):
        attend_back_chunk(r, c, False, (s,))
    for c in range(7):
        values_back(r, c, s)


def coarse_grad(r, kv, d, first, count, cols):
    base = d * D if kv else (ND + d) * D
    if cols is None:
        return r.gp[pl.ds(first, count), base : base + D]
    return r.gp[pl.ds(first, count), at_lanes(base, cols)]


def save_remote(r):
    for d in range(ND):
        last = []
        for kv in range(2):
            r.out5[2 * d + kv] = coarse_grad(r, kv, d, OFF[5], 16, None)
            last.append(coarse_grad(r, kv, d, OFF[6], 16, None).astype(f32))
        for j in range(2):
            rows = [v[j * 8 : j * 8 + 8] for v in last]
            r.back6[j, d] = jnp.concatenate(rows, axis=0).astype(bf16)


def coarse_rows(r, d, kv, s):
    keep = OFF[5] - LOC
    own = coarse_grad(r, kv, d, LOC, keep, s).astype(f32)
    lanes = pair_lanes(s)
    rest = jnp.zeros((LOC - keep - 24, 128), f32)
    far = r.far6[0, d, :, lanes].astype(f32) + r.far6[1, d, :, lanes].astype(f32)
    near = r.near5[2 * d + kv, :, lanes].astype(f32)
    return jnp.concatenate([own, near, far[kv * 8 : kv * 8 + 8], rest], axis=0)


def unpool(r, z, s):
    lanes = pair_lanes(s)
    for d in range(ND):
        q = r.gp[pl.ds(0, LOC), at_lanes((ND + d) * D, s)].astype(f32) * r.inv[ND]
        k = coarse_rows(r, d, 0, s) * r.inv[d]
        v = coarse_rows(r, d, 1, s)
        o = dot(r.unpool[...], jnp.concatenate([q, k, v], axis=1).astype(bf16))
        rows = pl.ds(d * LOC, LOC)
        fine = ext_rows(d, 0, LOC)
        live = iota((LOC, 128), 0) + z * LOC < r.lens[d]
        q = r.num[fine, lanes] + o[:, :128]
        r.gq[rows, lanes] = (q * (HD**-0.5)).astype(bf16)
        k = r.num[ext_rows(d, LOC, LOC), lanes] + o[:, 128:256]
        r.gk[rows, lanes] = jnp.where(live, k, 0.0).astype(bf16)
        v = r.gp[pl.ds(0, LOC), at_lanes(d * D, s)].astype(f32) + o[:, 256:]
        r.gv[rows, lanes] = jnp.where(live, v, 0.0).astype(bf16)


def attn_grads(r, s, k):
    lanes = pair_lanes(s)
    g = jnp.concatenate([r.gq[:, lanes], r.gk[:, lanes], r.gv[:, lanes]], axis=1)
    r.a_g[k, 0] = dot(r.h1[...], g, 0, 0).astype(bf16)


def input_grads(r, t):
    rows = rows_at(t, RT)
    gh1 = dot(r.gq[rows, :], attn_weight(r, 0), 1, 1)
    gh1 = gh1 + dot(r.gk[rows, :], attn_weight(r, 1), 1, 1)
    gh1 = gh1 + dot(r.gv[rows, :], attn_weight(r, 2), 1, 1)
    x = r.x[rows, :].astype(f32)
    r.gxs[rows, :] = r.gxs[rows, :] + norm_back(x, r.g1[...], gh1, r, 0)


def shard_of(z, k):
    return lax.rem(z + NMP - k, NMP)


def remote(src, dst, send, recv, where):
    return pltpu.make_async_remote_copy(
        src_ref=src, dst_ref=dst, send_sem=send, recv_sem=recv, device_id=where,
        device_id_type=pl.DeviceIdType.MESH,
    )


class Links:
    def __init__(self, r, ndp):
        self.r, self.ndp, self.nq, self.piece = r, ndp, ndp // 2, LOC // ndp
        self.z, self.me = lax.axis_index("mp"), lax.axis_index("dp")
        self.c, self.q = lax.rem(self.me, 2), self.me // 2
        self.other = 2 * self.q + 1 - self.c
        self.near = self.z + 1 - 2 * lax.rem(self.z, 2)
        self.far = (1 - self.z // 2) * 2
        self.par = lax.rem(self.z, 2)
        self.sent = []

    def mp_peer(self, k):
        return lax.rem(self.z + k, NMP)

    def dp_peer(self, k):
        return lax.rem(self.me + k, self.ndp)

    def quarter(self, j):
        return lax.rem(self.q + j, self.nq)

    def piece_rows(self, q):
        return pl.ds(pl.multiple_of(self.c * HALF + q * self.piece, self.piece), self.piece)

    def rows_of(self, dev):
        first = lax.rem(dev, 2) * HALF + (dev // 2) * self.piece
        return pl.ds(pl.multiple_of(first, self.piece), self.piece)

    def half(self, c):
        return pl.ds(pl.multiple_of(c * HALF, HALF), HALF)

    def send(self, src, dst, send, recv, where):
        copy = remote(src, dst, send, recv, where)
        copy.start()
        self.sent.append(copy)

    def arrive(self, dst, send, recv, where):
        remote(dst, dst, send, recv, where).wait_recv()

    def greet(self):
        sem = pltpu.get_barrier_semaphore()
        for k in range(1, NMP):
            pl.semaphore_signal(sem, inc=1, device_id={"mp": self.mp_peer(k)})
        for k in range(1, self.ndp):
            pl.semaphore_signal(sem, inc=1, device_id={"dp": self.dp_peer(k)})

    def barrier(self):
        pl.semaphore_wait(pltpu.get_barrier_semaphore(), NMP + self.ndp - 2)

    def gather_peers(self):
        for j in range(1, self.nq):
            yield self.quarter(j), self.piece_rows(self.quarter(self.nq - j))

    def part(self, m, shard, rows):
        w, cols = self.weights[m]
        return w.at[shard, :, rows, :] if cols is None else w.at[shard, rows, cols]

    def gather_z(self, m, k):
        i = m * 3 + k - 1
        piece = self.part(m, self.z, self.rows_of(self.me))
        self.send(piece, piece, self.r.wz_s.at[i], self.r.wz_r.at[i], {"mp": self.mp_peer(k)})

    def gather_plane(self, m, k):
        i = m * 3 + k - 1
        piece = self.part(m, shard_of(self.z, k), self.rows_of(self.me))
        self.arrive(piece, self.r.wz_s.at[i], self.r.wz_r.at[i], {"mp": self.mp_peer(k)})
        for j, (to, _) in enumerate(self.gather_peers()):
            n = i * (self.nq - 1) + j
            where = {"dp": 2 * to + self.c}
            self.send(piece, piece, self.r.wp_s.at[n], self.r.wp_r.at[n], where)

    def gather_core(self, m, k):
        i = m * 3 + k - 1
        shard = shard_of(self.z, k)
        for j, (to, rows) in enumerate(self.gather_peers()):
            n = i * (self.nq - 1) + j
            got = self.part(m, shard, rows)
            self.arrive(got, self.r.wp_s.at[n], self.r.wp_r.at[n], {"dp": 2 * to + self.c})
        start(self.gather_core_copies(m, k))

    def gather_core_copies(self, m, k):
        i = m * 3 + k - 1
        part = self.part(m, shard_of(self.z, k), self.half(self.c))
        return [remote(part, part, self.r.wc_s.at[i], self.r.wc_r.at[i], {"dp": self.other})]

    def gather_done(self, m, k):
        i = m * 3 + k - 1
        part = self.part(m, shard_of(self.z, k), self.half(1 - self.c))
        self.arrive(part, self.r.wc_s.at[i], self.r.wc_r.at[i], {"dp": self.other})

    def coarse_copies(self, here5, here6, there5, there6, sems):
        a, b = sems
        send = [remote(here5, there5, a.at[0], b.at[0], {"mp": self.near})]
        for j in range(2):
            where = {"mp": self.far + j}
            dst = there6.at[self.par]
            send.append(remote(here6[j], dst, a.at[1 + j], b.at[1 + self.par], where))
        return send

    def coarse_start(self, *args):
        self.coarse = self.coarse_copies(*args)
        start(self.coarse)

    def coarse_arrive(self, there5, there6, sems):
        a, b = sems
        self.arrive(there5, a.at[0], b.at[0], {"mp": self.near})
        for j in range(2):
            self.arrive(there6.at[j], a.at[1 + j], b.at[1 + j], {"mp": self.far + j})

    def coarse_send(self):
        r = self.r
        self.coarse_start(r.out5, (r.out6, r.out6), r.in5, r.in6, (r.cf_s, r.cf_r))

    def coarse_wait(self):
        r = self.r
        self.coarse_arrive(r.in5, r.in6, (r.cf_s, r.cf_r))

    def coarse_clear(self):
        for copy in self.coarse:
            copy.wait_send()

    def coarse_back(self):
        r = self.r
        here = (r.back6.at[0], r.back6.at[1])
        self.coarse_start(r.out5, here, r.near5, r.far6, (r.cb_s, r.cb_r))

    def coarse_back_wait(self):
        r = self.r
        self.coarse_arrive(r.near5, r.far6, (r.cb_s, r.cb_r))

    def norms_z(self):
        r = self.r
        r.nz[self.z] = r.norms[...]
        for k in range(1, NMP):
            dst = r.nz.at[self.z]
            where = {"mp": self.mp_peer(k)}
            self.send(r.norms, dst, r.nz_s.at[k - 1], r.nz_r.at[k - 1], where)

    def norms_dp(self):
        r = self.r
        for k in range(1, NMP):
            got = r.nz.at[self.mp_peer(NMP - k)]
            self.arrive(got, r.nz_s.at[k - 1], r.nz_r.at[k - 1], {"mp": self.mp_peer(k)})
        tot = r.nz[0]
        for k in range(1, NMP):
            tot = tot + r.nz[k]
        r.np[self.me] = tot
        for k in range(1, self.ndp):
            dst = r.np.at[self.me]
            where = {"dp": self.dp_peer(k)}
            self.send(dst, dst, r.np_s.at[k - 1], r.np_r.at[k - 1], where)

    def norms_done(self):
        r = self.r
        for k in range(1, self.ndp):
            got = r.np.at[self.dp_peer(self.ndp - k)]
            self.arrive(got, r.np_s.at[k - 1], r.np_r.at[k - 1], {"dp": self.dp_peer(k)})
        tot = r.np[0]
        for k in range(1, self.ndp):
            tot = tot + r.np[k]
        r.onorm[...] = tot

    def finish(self):
        wait(self.sent)
        self.sent = []

    def finish_cores(self):
        cores = [c for m in range(3) for k in (1, 2, 3) for c in self.gather_core_copies(m, k)]
        wait(cores)


def start(copies):
    for copy in copies:
        copy.start()


def wait(copies):
    for copy in copies:
        copy.wait_send()


class Sum:
    def __init__(self, net, r, name):
        self.net, self.together = net, name == "o"
        for n in ("g", "rc", "rp", "pz", "rz", "fin", "c_s", "c_r", "p_s", "p_r", "z_s", "z_r", "s_s", "s_r"):
            setattr(self, n, getattr(r, name + "_" + n))
        self.parts = self.g.shape[1]

    def core_copies(self, k):
        net = self.net
        src = self.g.at[k, :, net.half(1 - net.c), :]
        return [remote(src, self.rc.at[k], self.c_s.at[k], self.c_r.at[k], {"dp": net.other})]

    def plane_copies(self, k):
        net, copies = self.net, []
        for j in range(1, net.nq):
            n = k * (net.nq - 1) + j - 1
            to = net.quarter(j)
            src = self.g.at[k, :, net.piece_rows(to), :]
            where = {"dp": 2 * to + net.c}
            copies.append(remote(src, self.rp.at[k, j - 1], self.p_s.at[n], self.p_r.at[n], where))
        return copies

    def z_copies(self, k):
        where = {"mp": shard_of(self.net.z, k)}
        src, dst = self.pz.at[k - 1], self.rz.at[k - 1]
        return [remote(src, dst, self.z_s.at[k - 1], self.z_r.at[k - 1], where)]

    def share_copies(self):
        net, copies = self.net, []
        part = self.fin.at[:, net.rows_of(net.me), :]
        for j in range(1, net.nq):
            where = {"dp": 2 * net.quarter(j) + net.c}
            copies.append(remote(part, part, self.s_s.at[j - 1], self.s_r.at[j - 1], where))
        return copies

    def share_core_copies(self):
        net = self.net
        n = net.nq - 1
        part = self.fin.at[:, net.half(net.c), :]
        return [remote(part, part, self.s_s.at[n], self.s_r.at[n], {"dp": net.other})]

    def all_core_copies(self):
        net = self.net
        src = self.g.at[:, :, net.half(1 - net.c), :]
        return [remote(src, self.rc, self.c_s.at[0], self.c_r.at[0], {"dp": net.other})]

    def all_plane_copies(self):
        net, copies = self.net, []
        for j in range(1, net.nq):
            to = net.quarter(j)
            src = self.g.at[:, :, net.piece_rows(to), :]
            where = {"dp": 2 * to + net.c}
            sems = self.p_s.at[j - 1], self.p_r.at[j - 1]
            copies.append(remote(src, self.rp.at[:, j - 1], *sems, where))
        return copies

    def all_core(self):
        start(self.all_core_copies())

    def all_plane(self):
        net = self.net
        net.arrive(self.rc, self.c_s.at[0], self.c_r.at[0], {"dp": net.other})
        for k in range(NMP):
            self.add_half(k)
        start(self.all_plane_copies())

    def all_pass_on(self):
        net = self.net
        for j in range(1, net.nq):
            where = {"dp": 2 * net.quarter(j) + net.c}
            net.arrive(self.rp.at[:, j - 1], self.p_s.at[j - 1], self.p_r.at[j - 1], where)
        for k in range(1, NMP):
            self.pass_on(k)

    def core(self, k):
        start(self.core_copies(k))

    def plane(self, k):
        net = self.net
        net.arrive(self.rc.at[k], self.c_s.at[k], self.c_r.at[k], {"dp": net.other})
        self.add_half(k)
        start(self.plane_copies(k))

    def add_half(self, k):
        net = self.net

        def add(i):
            a, b = i // 2, lax.rem(i, 2)
            rows = pl.ds(pl.multiple_of(net.c * HALF + b * 128, 128), 128)
            more = self.rc[k, a, rows_at(b, 128), :].astype(f32)
            self.g[k, a, rows, :] = (self.g[k, a, rows, :].astype(f32) + more).astype(bf16)

        loop(2 * self.parts, add)

    def total(self, k):
        net = self.net
        for j in range(1, net.nq if not self.together else 1):
            n = k * (net.nq - 1) + j - 1
            where = {"dp": 2 * net.quarter(j) + net.c}
            net.arrive(self.rp.at[k, j - 1], self.p_s.at[n], self.p_r.at[n], where)
        tots = []
        for a in range(self.parts):
            tot = self.g[k, a, net.piece_rows(net.q), :].astype(f32)
            for j in range(net.nq - 1):
                tot = tot + self.rp[k, j, a].astype(f32)
            tots.append(tot)
        return tots

    def pass_on(self, k):
        for a, tot in enumerate(self.total(k)):
            self.pz[k - 1, a] = tot.astype(bf16)
        start(self.z_copies(k))

    def share(self):
        net = self.net
        tots = self.total(0)
        for k in range(1, NMP):
            where = {"mp": shard_of(net.z, k)}
            net.arrive(self.rz.at[k - 1], self.z_s.at[k - 1], self.z_r.at[k - 1], where)
            tots = [tot + self.rz[k - 1, a].astype(f32) for a, tot in enumerate(tots)]
        mine = net.rows_of(net.me)
        for a, tot in enumerate(tots):
            self.fin[a, mine, :] = tot.astype(bf16)
        start(self.share_copies())

    def share_core(self):
        net = self.net
        for j in range(1, net.nq):
            got = self.fin.at[:, net.piece_rows(net.quarter(net.nq - j)), :]
            where = {"dp": 2 * net.quarter(j) + net.c}
            net.arrive(got, self.s_s.at[j - 1], self.s_r.at[j - 1], where)
        start(self.share_core_copies())

    def done(self):
        net = self.net
        n = net.nq - 1
        part = self.fin.at[:, net.half(1 - net.c), :]
        net.arrive(part, self.s_s.at[n], self.s_r.at[n], {"dp": net.other})

    def finish(self):
        if self.together:
            wait(self.all_core_copies() + self.all_plane_copies())
        else:
            loop(NMP, lambda k: wait(self.core_copies(k) + self.plane_copies(k)))
        wait([copy for k in range(1, NMP) for copy in self.z_copies(k)])

    def finish_share(self):
        wait(self.share_copies() + self.share_core_copies())


def whole_kernel(ndp, r):
    net = Links(r, ndp)
    r.wup, r.wdn = r.wff.at[:, 0], r.wff.at[:, 1]
    z = net.z
    r.gq, r.gk, r.gv = (e.at[pl.ds(0, T), :] for e in (r.qe, r.ke, r.ve))
    net.weights = (
        (r.wat, pl.ds(0, 384)),
        (r.wff, None),
        (r.wat, pl.ds(384, 128)),
    )
    r.mx, r.gof = r.h2, r.pool
    r.fa, r.fb = r.tops, r.sumz
    net_f, net_o, net_a = (Sum(net, r, n) for n in "foa")
    shard = [shard_of(z, k) for k in range(NMP)]
    loads = [pltpu.make_async_copy(r.x_in, r.raw, r.ld.at[0])]
    for i, w in enumerate((r.w_query, r.w_key, r.w_value)):
        dst = r.wat.at[z, :, pl.ds(i * 128, 128)]
        loads.append(pltpu.make_async_copy(w, dst, r.ld.at[1 + i]))
    loads.append(pltpu.make_async_copy(r.w_up, r.wup.at[z], r.ld.at[4]))
    loads.append(pltpu.make_async_copy(r.w_down, r.wdn.at[z], r.ld.at[5]))
    start(loads)
    net.greet()
    loads[0].wait()
    by_document(r.x, r.raw)
    load_gy = pltpu.make_async_copy(r.gy_in, r.raw, r.ld.at[6])
    load_gy.start()
    norm_one(r)
    r.wat[z, :, pl.ds(384, 128)] = r.w_output[...].T
    for copy in loads[1:4]:
        copy.wait()
    net.barrier()
    for m in (0, 2):
        for k in (1, 2, 3):
            net.gather_z(m, k)
    for copy in loads[4:]:
        copy.wait()
    build_tables(r, z, 0)
    build_tables(r, z, 1)
    net.gather_z(1, 1)
    for k in (1, 2, 3):
        net.gather_plane(0, k)
    for k in (1, 2, 3):
        net.gather_plane(2, k)
    net.gather_z(1, 2)
    build_maps(r)
    project(r, z, shard[:1])
    pool_levels(r, shard[:1])
    net.gather_z(1, 3)
    for k in (1, 2, 3):
        net.gather_core(0, k)
    attend_own(r, shard[0])
    net.gather_plane(1, 1)
    for k in (1, 2, 3):
        net.gather_done(0, k)
    project(r, z, shard[1:])
    for k in (1, 2, 3):
        net.gather_core(2, k)
    pool_levels(r, shard[1:])
    net.coarse_send()
    net.gather_plane(1, 2)
    for c in range(7):
        attend_chunk(r, c, shard[1:])
        if c == 2:
            net.gather_plane(1, 3)
    net.coarse_wait()
    net.coarse_clear()
    place_remote(r)
    attend_chunk(r, EXT // 128 - 1, range(NMP))
    combine_sums(r)
    load_gy.wait()
    by_document(r.gy, r.raw)
    combine_values(r)
    for k in (1, 2, 3):
        net.gather_done(2, k)
    attn_out(r)

    def ffn_step(k):
        f = shard_of(z, k)

        @pl.when(k > 0)
        def _():
            net.gather_done(1, k)

        ffn_inner(r, f)

        @pl.when(k < NMP - 1)
        def _():
            net.gather_core(1, k + 1)

        ffn_grads(r, f, k)
        net_f.core(k)

        @pl.when(k > 0)
        def _():
            net_f.plane(k - 1)

    loop(NMP, ffn_step)
    ffn_outer(r, 0)
    net_f.plane(3)
    ffn_outer(r, 1)
    put_mixed = pltpu.make_async_copy(r.mx, r.mixed, r.st.at[0])
    put_mixed.start()
    out_grads(r, z)
    net_o.all_core()
    context_grads(r)
    attn_back_rows(r)
    net_f.pass_on(1)
    net_o.all_plane()
    attend_back_chunk(r, EXT // 128 - 1, False, range(NMP))
    for s in range(NMP):
        values_back(r, 7, s)
    save_remote(r)
    net.coarse_back()

    def back_step(i):
        k = lax.rem(i + 1, NMP)
        s = shard_of(z, k)
        attend_back_pair(r, s)

        @pl.when(i == 0)
        def _():
            net.coarse_back_wait()

        unpool(r, z, s)

        attn_grads(r, s, k)
        net_a.core(k)

        @pl.when(i > 0)
        def _():
            net_a.plane(i)

        @pl.when(i == 0)
        def _():
            net_f.pass_on(2)

        @pl.when(i == 1)
        def _():
            net_f.pass_on(3)
            net_o.all_pass_on()

        @pl.when(i == 2)
        def _():
            net_f.share()

        @pl.when(i == 3)
        def _():
            net_o.share()

        @pl.when(i > 1)
        def _():
            net_a.pass_on(i - 1)

    loop(NMP, back_step)
    input_grads(r, 0)
    net_a.plane(0)
    net_o.share_core()
    net_f.share_core()
    input_grads(r, 1)
    net_a.pass_on(3)
    net.finish()
    net.norms_z()
    put_gx = pltpu.make_async_copy(r.gxs, r.gx, r.st.at[1])
    put_gx.start()
    net.coarse_clear()
    net.finish_cores()
    for each in (net_f, net_o):
        each.finish()
    net_f.done()
    net_o.done()
    stores = [put_mixed, put_gx]
    for i, (a, b) in enumerate(((r.f_fin, r.ofn), (r.o_fin, r.oot), (r.a_fin, r.oat))):
        stores.append(pltpu.make_async_copy(a, b, r.st.at[2 + i]))
    start(stores[2:4])
    net_a.share()
    net.norms_dp()
    net_a.share_core()
    net.norms_done()
    net_a.done()
    start(stores[4:])
    for copy in stores:
        copy.wait()
    net_a.finish()
    for each in (net_f, net_o, net_a):
        each.finish_share()
    net.finish()


FAR_OUTS = ("mixed", "gx", "ofn", "oot", "oat")


def run(body, ins, outs, scratch, sems):
    names = list(ins) + list(outs) + list(scratch) + list(sems)

    def kernel(*refs):
        body(types.SimpleNamespace(**dict(zip(names, refs))))

    result = pl.pallas_call(
        kernel,
        out_shape=[jax.ShapeDtypeStruct(*v) for v in outs.values()],
        in_specs=[pl.BlockSpec(memory_space=space) for _, space in ins.values()],
        out_specs=[
            pl.BlockSpec(memory_space=pl.ANY if n in FAR_OUTS else pltpu.VMEM) for n in outs
        ],
        scratch_shapes=[pltpu.VMEM(*v) for v in scratch.values()]
        + [pltpu.SemaphoreType.DMA((n,)) for n in sems.values()],
        compiler_params=pltpu.CompilerParams(
            vmem_limit_bytes=63 * 1024 * 1024, collective_id=0, has_side_effects=True
        ),
    )(*[a for a, _ in ins.values()])
    return dict(zip(outs, result))


def per_device(
    ndp,
    tokens,
    lengths,
    gain_one,
    shift_one,
    w_query,
    w_key,
    w_value,
    w_output,
    gain_two,
    shift_two,
    w_up,
    w_down,
    cotangent,
):
    g1, b1, g2, b2 = (v.reshape(1, D) for v in (gain_one, shift_one, gain_two, shift_two))
    nq, piece = ndp // 2, LOC // ndp
    vmem, any_space = pltpu.VMEM, pl.ANY
    ins = dict(
        lens=(lengths, pltpu.SMEM),
        x_in=(tokens, any_space),
        gy_in=(cotangent, any_space),
        g1=(g1, vmem),
        b1=(b1, vmem),
        g2=(g2, vmem),
        b2=(b2, vmem),
        w_query=(w_query, any_space),
        w_key=(w_key, any_space),
        w_value=(w_value, any_space),
        w_output=(w_output, vmem),
        w_up=(w_up, any_space),
        w_down=(w_down, any_space),
    )
    outs = dict(
        mixed=((T, D), bf16),
        gx=((T, D), f32),
        ofn=((2, D, 512), bf16),
        oot=((1, D, 128), bf16),
        oat=((1, D, 384), bf16),
        onorm=((8, D), f32),
    )
    scratch = dict(
        x=((T, D), bf16),
        gy=((T, D), bf16),
        gxs=((T, D), f32),
        inv=((ND + 1, EXT - LOC, 128), f32),
        wat=((NMP, D, 512), bf16),
        wff=((NMP, 2, 512, 512), bf16),
        h1=((T, D), bf16),
        qe=((ND * EXT, D), bf16),
        ke=((ND * EXT, D), bf16),
        ve=((ND * EXT, D), bf16),
        pool=((EXT - LOC, LOC), bf16),
        unpool=((LOC, EXT - LOC), bf16),
        cc=((ND * EXT, 128), bf16),
        bias=((ND * EXT, 128), bf16),
        wts=((64 * 128, 256), bf16),
        num=((ND * EXT, D), f32),
        tops=((EXT, 128), f32),
        sumz=((EXT, 128), f32),
        up=((LOC, 128), f32),
        up2=((LOC, 128), f32),
        ctx=((T, D), bf16),
        h2=((T, D), bf16),
        act=((T, FF), bf16),
        gp=((T, FF), bf16),
        gm=((T, D), bf16),
        hc=((T // 2, D), f32),
        dl=((EXT, 128), f32),
        ee=((ND, 256, D), bf16),
        crow=((ND * EXT // 128, 128), f32),
        raw=((LOC, ND, D), bf16),
        out5=((2 * ND, 16, D), bf16),
        out6=((ND, 16, D), bf16),
        in5=((2 * ND, 16, D), bf16),
        in6=((2, ND, 16, D), bf16),
        back6=((2, ND, 16, D), bf16),
        near5=((2 * ND, 16, D), bf16),
        far6=((2, ND, 16, D), bf16),
        norms=((8, D), f32),
        nz=((NMP, 8, D), f32),
        np=((ndp, 8, D), f32),
    )
    counts = dict(wz=9, wp=9 * (nq - 1), wc=9, cf=3, cb=3, nz=3, np=ndp - 1)
    for n, a, cols in (("f", 2, 512), ("o", 1, 128), ("a", 1, 384)):
        scratch[n + "_g"] = ((NMP, a, 512, cols), bf16)
        scratch[n + "_rc"] = ((NMP, a, HALF, cols), bf16)
        scratch[n + "_rp"] = ((NMP, nq - 1, a, piece, cols), bf16)
        scratch[n + "_pz"] = ((NMP - 1, a, piece, cols), bf16)
        scratch[n + "_rz"] = ((NMP - 1, a, piece, cols), bf16)
        scratch[n + "_fin"] = ((a, 512, cols), bf16)
        counts.update({n + "_c": NMP, n + "_p": NMP * (nq - 1), n + "_z": NMP - 1, n + "_s": nq})
    sems = dict(ld=7, st=5)
    for n, count in counts.items():
        sems[n + "_s"] = count
        sems[n + "_r"] = count
    o = run(lambda r: whole_kernel(ndp, r), ins, outs, scratch, sems)

    outs = emit(o)
    return outs


def emit_kernel(mixed, gx, fn, at, ot, norms, o_mixed, o_gx, o_q, o_k, o_v, o_o, o_up, o_dn, *o_norms):
    for i, out in enumerate(o_norms):
        out[...] = norms[i, :]
    for d in range(ND):
        o_mixed[:, d, :] = mixed[d]
        o_gx[:, d, :] = gx[d]
    for i, out in enumerate((o_q, o_k, o_v)):
        out[...] = at[0, :, i * 128 : (i + 1) * 128].astype(f32)
    o_up[...] = fn[0].astype(f32)
    o_dn[...] = fn[1].astype(f32)
    o_o[...] = ot[0].astype(f32).T


def emit(o):
    n = 2
    rows = LOC // n

    def tiles(*shape, axis):
        block = tuple(rows if i == axis else size for i, size in enumerate(shape))
        return pl.BlockSpec(block, lambda i: tuple(i if a == axis else 0 for a in range(len(shape))))

    doc = tiles(ND, LOC, D, axis=1)
    pos = tiles(LOC, ND, D, axis=0)
    third, whole = tiles(512, 128, axis=0), tiles(512, D, axis=0)
    shape = jax.ShapeDtypeStruct
    return pl.pallas_call(
        emit_kernel,
        grid=(n,),
        in_specs=[
            doc,
            doc,
            tiles(2, 512, 512, axis=1),
            tiles(1, 512, 384, axis=1),
            tiles(1, 512, 128, axis=1),
            tiles(8, D, axis=None),
        ],
        out_specs=[pos, pos, third, third, third, tiles(128, D, axis=1), whole, whole]
        + [tiles(D, axis=None)] * 4,
        out_shape=[shape((LOC, ND, D), bf16), shape((LOC, ND, D), f32)]
        + [shape((D, 128), f32)] * 3
        + [shape((128, D), f32), shape((D, 512), f32), shape((512, D), f32)]
        + [shape((D,), f32)] * 4,
    )(o["mixed"].reshape(ND, LOC, D), o["gx"].reshape(ND, LOC, D), o["ofn"], o["oat"], o["oot"], o["onorm"])


def solution(mesh):
    tok = P("mp", "dp", None)
    col, row, rep = P(None, "mp"), P("mp", None), P()
    ndp = mesh.shape["dp"]
    return jax.shard_map(
        lambda *args: per_device(ndp, *args),
        mesh=mesh,
        in_specs=(tok, P("dp"), rep, rep, col, col, col, row, rep, rep, col, row, tok),
        out_specs=(tok, tok, col, col, col, row, col, row, rep, rep, rep, rep),
        check_vma=False,
    )
```
